512 devices in a mesh: gz: 64 (over y, z), xy: 8 (over x, core).
Axes of the slice: x: 4, y: 4, z: 16, core: 2. Of those that a mesh axis runs over, the one named last changes fastest.
Arguments:
- right_side: float32 [2, 64, 64, 2048], P(None, 'gz', 'xy')
- stiff_across: float32 [64, 64, 2048], P('gz', 'xy'), may hold values from 0.3 to 3
- stiff_down: float32 [64, 64, 2048], P('gz', 'xy'), may hold values from 0.3 to 3
- anchor: float32 [64, 64, 2048], P('gz', 'xy'), may hold values from 0.02 to 0.2
- source_node: int32 [64, 8, 1024], P('gz', 'xy'), may hold values from 0 to 16383
- target_cell: int32 [64, 8, 1024], P('gz', 'xy'), may hold values from 0 to 14334, as said below
- corner_weight: float32 [4, 64, 8, 1024], P(None, 'gz', 'xy'), may hold values from 0 to 1, as said below
- block_count: int32 [64, 8], P('gz', 'xy'), may hold values from 1 to 8, as said below
Outputs:
- solution_field: float32 [2, 64, 64, 2048], P(None, 'gz', 'xy')
- residual: float32 [2, 64, 64, 2048], P(None, 'gz', 'xy')
The draws below stay inside these ranges and needn't reach their ends.
Inputs may be any that keep to these rules, and one draw needn't show every extreme that they name: `target_cell`: each target cell's row is below 7 and its column below 2047 within the block, so all four corners lie in the same block. `corner_weight`: the weights of a slot are nonnegative and sum to 1. `block_count`: some device holds exactly 8 used blocks.
All inputs are finite; a program needn't handle non-finite values.
Results may differ from the reference program's by a relative error of at most 0.00013.
Values sent between devices are 32-bit elements; how exact they have to be, the bound alone decides.
A program may use at most 64 MiB of HBM per device.

```python
import math
import jax
import jax.numpy as jnp

COLS = 2048
R_DEV = 8
BLOCK = 128
MAXB = 8
ITERS = 3
SECTIONS = 64
ROWS = 64
CORR = 1024
N_XY = 8


def draw_right_side(key, part):
    shape = (2, SECTIONS, R_DEV * N_XY, COLS)
    ramp = 1.0 + 2.0 * jnp.arange(SECTIONS, dtype=jnp.float32) / max(SECTIONS - 1, 1)
    values = jnp.clip(jax.random.normal(jax.random.fold_in(key, 12), shape, jnp.float32), -6.0, 6.0)
    values = values * ramp[None, :, None, None]
    return values.astype(jnp.float32)


def draw_target_cell(key, part):
    first, second = jax.random.split(jax.random.fold_in(key, 21))
    shape = (SECTIONS, N_XY, MAXB * BLOCK)
    row = jax.random.randint(first, shape, 0, R_DEV - 1)
    column = jax.random.randint(second, shape, 0, COLS - 1)
    return (row * COLS + column).astype(jnp.int32)


def draw_corner_weight(key, part):
    first, second = jax.random.split(jax.random.fold_in(key, 31))
    shape = (SECTIONS, N_XY, MAXB * BLOCK)
    across = jax.random.uniform(first, shape, jnp.float32)
    down = jax.random.uniform(second, shape, jnp.float32)
    return jnp.stack([(1.0 - across) * (1.0 - down), across * (1.0 - down), (1.0 - across) * down, across * down]).astype(jnp.float32)


def draw_block_count(key, part):
    first, second, third = jax.random.split(jax.random.fold_in(key, 41), 3)
    shape = (SECTIONS * N_XY,)
    one = jax.random.randint(first, shape, 0, MAXB)
    two = jax.random.randint(second, shape, 0, MAXB)
    counts = 1 + one * two // MAXB
    where = jax.random.randint(third, (), 0, SECTIONS * N_XY)
    counts = counts.at[where].set(MAXB)
    return counts.reshape(SECTIONS, N_XY).astype(jnp.int32)


def with_ends(values, key, smallest, largest):
    index_at = [jax.random.randint(jax.random.fold_in(key, axis), (), 0, length) for axis, length in enumerate(values.shape)]
    longest = values.shape.index(max(values.shape))
    neighbour = index_at[:longest] + [(index_at[longest] + 1) % values.shape[longest]] + index_at[longest + 1:]
    return values.at[tuple(index_at)].set(smallest).at[tuple(neighbour)].set(largest)


def block_scale(own_key, shape, pieces, low, high):
    def one(axis_at, shards_of):
        heights = jax.random.uniform(jax.random.fold_in(jax.random.fold_in(own_key, 6), axis_at), (shards_of,), jnp.float32, low / len(pieces), high / len(pieces))
        return jnp.repeat(jnp.exp(heights), shape[axis_at] // shards_of).reshape((-1,) + (1,) * (len(shape) - axis_at - 1))

    level = one(*pieces[0])
    for cut in pieces[1:]:
        level = level * one(*cut)
    return level


def setup_inputs(seed: int = 0) -> dict:
    key_of = jax.random.split(jax.random.key(seed), 9)
    right_side = draw_right_side(jax.random.fold_in(key_of[8], 71), 0)
    stiff_across = jnp.clip(jnp.exp(math.log(3.0) - 2.3025851 * jax.random.uniform(key_of[1], (SECTIONS, ROWS, COLS), jnp.float32) ** block_scale(key_of[1], (SECTIONS, ROWS, COLS), ((0, 64), (1, 8)), -0.2, 0.2)), 0.3, 3.0)
    stiff_down = jnp.clip(jnp.exp(math.log(3.0) - 2.3025851 * jax.random.uniform(key_of[2], (SECTIONS, ROWS, COLS), jnp.float32) ** block_scale(key_of[2], (SECTIONS, ROWS, COLS), ((0, 64), (1, 8)), -0.2, 0.2)), 0.3, 3.0)
    anchor = jnp.clip(jnp.exp(math.log(0.2) - 2.3025851 * jax.random.uniform(key_of[3], (SECTIONS, ROWS, COLS), jnp.float32) ** block_scale(key_of[3], (SECTIONS, ROWS, COLS), ((0, 64), (1, 8)), -0.2, 0.2)), 0.02, 0.2)
    source_node = with_ends(jax.random.randint(key_of[4], (SECTIONS, N_XY, CORR), 0, R_DEV * COLS), jax.random.fold_in(key_of[4], 1), 0, (R_DEV * COLS) - 1).astype(jnp.int32)
    target_cell = draw_target_cell(jax.random.fold_in(key_of[8], 71), 0)
    corner_weight = draw_corner_weight(jax.random.fold_in(key_of[8], 71), 0)
    block_count = draw_block_count(jax.random.fold_in(key_of[8], 71), 0)
    return {"right_side": right_side, "stiff_across": stiff_across, "stiff_down": stiff_down, "anchor": anchor, "source_node": source_node, "target_cell": target_cell, "corner_weight": corner_weight, "block_count": block_count}


def springs(field, across, down, hold):
    zero_col = jnp.zeros(field.shape[:-1] + (1,), field.dtype)
    zero_row = jnp.zeros(field.shape[:-2] + (1, field.shape[-1]), field.dtype)
    right = jnp.concatenate([field[..., 1:], zero_col], -1)
    left = jnp.concatenate([zero_col, field[..., :-1]], -1)
    lower = jnp.concatenate([field[..., 1:, :], zero_row], -2)
    upper = jnp.concatenate([zero_row, field[..., :-1, :]], -2)
    across_left = jnp.concatenate([jnp.zeros(across.shape[:-1] + (1,), across.dtype), across[..., :-1]], -1)
    down_above = jnp.concatenate([jnp.zeros(down.shape[:-2] + (1, down.shape[-1]), down.dtype), down[..., :-1, :]], -2)
    return (across * (field - right) + across_left * (field - left)
            + down * (field - lower) + down_above * (field - upper) + hold * field)


def reference(right_side, stiff_across, stiff_down, anchor, source_node, target_cell, corner_weight, block_count):
    block_size = R_DEV * COLS
    total = SECTIONS * N_XY * block_size
    base = ((jnp.arange(SECTIONS, dtype=jnp.int32)[:, None] * N_XY
             + jnp.arange(N_XY, dtype=jnp.int32)[None, :]) * block_size).astype(jnp.int32)
    source_all = (source_node + base[:, :, None]).reshape(-1).astype(jnp.int32)
    offsets = jnp.array([0, 1, COLS, COLS + 1], dtype=jnp.int32)
    corners_all = (target_cell[None] + offsets[:, None, None, None] + base[None, :, :, None]
                   + N_XY * block_size).astype(jnp.int32)
    corners_all = jnp.minimum(corners_all, total - 1).reshape(4, -1).astype(jnp.int32)
    weights = corner_weight.reshape(4, -1)
    slot = jnp.arange(CORR, dtype=jnp.int32)
    live = (slot[None, None, :] < block_count[:, :, None] * BLOCK) & (jnp.arange(SECTIONS, dtype=jnp.int32) < SECTIONS - 1)[:, None, None]
    live = live.reshape(-1).astype(right_side.dtype)

    def operate(field):
        flat = field.reshape(2, -1)
        interp = jnp.sum(weights[None] * flat[:, corners_all], 1)
        error = (interp - flat[:, source_all]) * live[None]
        result = jnp.zeros_like(flat).at[:, source_all].add(-error)
        result = result.at[:, corners_all.reshape(-1)].add((weights[None] * error[:, None, :]).reshape(2, -1))
        return springs(field, stiff_across, stiff_down, anchor) + result.reshape(field.shape)

    solution_field = jnp.zeros_like(right_side)
    residual, direction = right_side, right_side
    norm_now = jnp.sum(residual * residual)
    for step in range(ITERS):
        image = operate(direction)
        alpha = norm_now / jnp.sum(direction * image)
        solution_field = solution_field + alpha * direction
        residual = residual - alpha * image
        norm_next = jnp.sum(residual * residual)
        direction = residual + (norm_next / norm_now) * direction
        norm_now = norm_next
    return solution_field, residual
```

```python
import functools

import jax
import jax.numpy as jnp
from jax import lax
from jax.experimental import pallas as pl
from jax.experimental.pallas import tpu as pltpu
from jax.sharding import PartitionSpec as P

BLOCK = 128
ITERS = 3
LOW = 256
SCALE = 8.0
MESH = pl.DeviceIdType.MESH
MOMENTS = 2 * ITERS


def pieces(values, count):
    out = []
    for i in range(count):
        part = values.astype(jnp.bfloat16)
        out.append(part)
        if i + 1 < count:
            values = values - part.astype(jnp.float32)
    return jnp.concatenate(out, 0)


def summed(pieces_of, count):
    rows = pieces_of.shape[0] // count
    total = pieces_of[:rows]
    for i in range(1, count):
        total = total + pieces_of[i * rows : (i + 1) * rows]
    return total


def stacked(field):
    return jnp.concatenate(
        [part[:, h : h + LOW] for part in field for h in range(0, part.shape[1], LOW)], 0
    )


def unstacked(table, rows, highs):
    return [
        jnp.concatenate(
            [table[(c * highs + h) * rows : (c * highs + h + 1) * rows] for h in range(highs)], 1
        )
        for c in range(2)
    ]


def looked_up(table, hot, masks, first):
    wide = hot.shape[1]
    cut = min(wide, 256)
    out = []
    for j in range(0, wide, cut):
        found = jnp.dot(table, hot[:, j : j + cut], preferred_element_type=jnp.float32)
        out.append([])
        per = found.shape[0] // len(masks)
        totals = None
        for m, mask in enumerate(masks):
            got = summed(found[m * per : (m + 1) * per], first)
            half = got.shape[0] // 2
            terms = [got[c * half : (c + 1) * half] * mask[:, j : j + cut] for c in range(2)]
            totals = terms if totals is None else [a + b for a, b in zip(totals, terms)]
        out[-1] = [jnp.sum(t, 0, keepdims=True) for t in totals]
    return [jnp.concatenate([o[c] for o in out], 1) for c in range(2)]


def spread(errors, mask, hot, count):
    table = jnp.concatenate([mask[...] * e for e in errors], 0)
    out = lax.dot_general(
        pieces(table, count), hot[...], (((1,), (1,)), ((), ())), preferred_element_type=jnp.float32
    )
    return summed(out, count)


def folded(values):
    return sum(values[:, i : i + 128] for i in range(0, values.shape[1], 128))


def coefficients(mu):
    def inner(a, b, shift):
        total = None
        for i, x in enumerate(a):
            for j, y in enumerate(b):
                term = mu[i + j + shift]
                if x is not None:
                    term = x * term
                if y is not None:
                    term = y * term
                total = term if total is None else total + term
        return total

    residual, direction, field = [None], [None], []
    norm = mu[0]
    for step in range(ITERS):
        alpha = norm / inner(direction, direction, 1)
        along = [alpha if d is None else alpha * d for d in direction]
        field = [a if i >= len(field) else field[i] + a for i, a in enumerate(along)]
        residual = residual[:1] + [
            -a if i + 1 >= len(residual) else residual[i + 1] - a for i, a in enumerate(along)
        ]
        if step + 1 < ITERS:
            fresh = inner(residual, residual, 0)
            ratio = fresh / norm
            step_of = [ratio if d is None else ratio * d for d in direction]
            direction = [
                (1.0 if r is None else r) + (step_of[i] if i < len(step_of) else 0.0)
                for i, r in enumerate(residual)
            ]
            norm = fresh
    return field, residual


def kernel(
    ny,
    nz,
    nx,
    rhs_ref,
    across_ref,
    down_ref,
    anchor_ref,
    source_ref,
    target_ref,
    weight_ref,
    count_ref,
    x_ref,
    r_ref,
    hot_source,
    hot_target,
    mask_source,
    mask_left,
    mask_right,
    basis,
    weight_out,
    rim_out,
    halo_out,
    point_out,
    target_in,
    weight_in,
    rim_in,
    halo_in,
    point_in,
    sums,
    send_sem,
    recv_sem,
):
    rows, cols = across_ref.shape[1:]
    slots = source_ref.shape[2]
    highs = cols // LOW
    bits_cols, bits_low = cols.bit_length() - 1, LOW.bit_length() - 1
    n_gz = ny * nz
    gz, xy = lax.axis_index("gz"), lax.axis_index("xy")
    y, z = gz // nz, gz % nz
    after, before = ((gz + 1) % n_gz, xy), ((gz + n_gz - 1) % n_gz, xy)
    below, above = (gz, (xy + 1) % nx), (gz, (xy + nx - 1) % nx)

    groups = [[], [], []]
    for i in range(1, nx):
        groups[0].append((gz, (xy + i) % nx))
    for i in range(1, 2 * ny):
        groups[1].append((((y + i // 2) % ny) * nz + z - z % 2 + (z % 2 + i % 2) % 2, xy))
    for i in range(1, nz // 2):
        groups[2].append((y * nz + (z + 2 * i) % nz, xy))

    barrier = pltpu.get_barrier_semaphore()
    met = [after, before] + [peer for group in groups for peer in group]
    for peer in met:
        pl.semaphore_signal(barrier, inc=1, device_id=peer, device_id_type=MESH)

    sent = []

    def send(src, dst, peer, index):
        copy = pltpu.make_async_remote_copy(
            src_ref=src,
            dst_ref=dst,
            send_sem=send_sem.at[index],
            recv_sem=recv_sem.at[index],
            device_id=peer,
            device_id_type=MESH,
        )
        copy.start()
        sent.append(copy)
        return copy

    slot = lax.broadcasted_iota(jnp.int32, (1, slots), 1)
    live = ((slot < count_ref[0, 0] * BLOCK) & (gz < n_gz - 1)).astype(jnp.float32)
    for k in range(4):
        weight_out[k] = weight_ref[k, 0] * live
    rim_out[...] = down_ref[0, rows - 1 :]

    def post_halo(field, k):
        for c in range(2):
            halo_out[k, 0, c : c + 1, :] = field[c][:1]
            halo_out[k, 1, c : c + 1, :] = field[c][rows - 1 :]

    field = [rhs_ref[c, 0] for c in range(2)]
    post_halo(field, 0)

    low_id = lax.broadcasted_iota(jnp.int32, (LOW, slots), 0)
    place_id = lax.broadcasted_iota(jnp.int32, (highs * rows, slots), 0)

    def split(node):
        col = node & (cols - 1)
        return col & (LOW - 1), (col >> bits_low) * rows + (node >> bits_cols)

    low, place = split(source_ref[0])
    hot_source[...] = (low_id == low).astype(jnp.float32).astype(jnp.bfloat16)
    mask_source[...] = jnp.where(place_id == place, live, 0.0)

    pl.semaphore_wait(barrier, len(met))

    copies = [
        send(target_ref, target_in, after, 0),
        send(weight_out, weight_in, after, 1),
        send(rim_out, rim_in, below, 2),
    ]
    across, down, anchor = across_ref[0], down_ref[0], anchor_ref[0]
    col_id = lax.broadcasted_iota(jnp.int32, (rows, cols), 1)
    row_id = lax.broadcasted_iota(jnp.int32, (rows, cols), 0)
    products = [sum(folded(f * f) for f in field)]

    for k in range(ITERS):
        base = 3 + 4 * k
        halo = [
            send(halo_out.at[k, 0], halo_in.at[k, 0], above, base),
            send(halo_out.at[k, 1], halo_in.at[k, 1], below, base + 1),
        ]
        own = looked_up(pieces(stacked(field), 3), hot_source, [mask_source], 3)
        for c in range(2):
            point_out[k, 0, c : c + 1, :] = own[c]
        own_copy = send(point_out.at[k, 0], point_in.at[k, 0], after, base + 2)
        right = [jnp.where(col_id == cols - 1, 0.0, pltpu.roll(f, cols - 1, 1)) for f in field]
        if k == 0:
            copies[0].wait_recv()
            copies[1].wait_recv()
            low, place = split(target_in[0])
            hot_target[...] = (low_id == low).astype(jnp.float32).astype(jnp.bfloat16)
            for mask, one, two in ((mask_left, 0, 2), (mask_right, 1, 3)):
                mask[...] = jnp.where(
                    place_id == place,
                    weight_in[one],
                    jnp.where(place_id == place + 1, weight_in[two], 0.0),
                )
        table = jnp.concatenate([pieces(stacked(field), 3), pieces(stacked(right), 3)], 0)
        there = looked_up(table, hot_target, [mask_left, mask_right], 3)
        for c in range(2):
            point_out[k, 1, c : c + 1, :] = there[c]
        there_copy = send(point_out.at[k, 1], point_in.at[k, 1], before, base + 3)

        if k == 0:
            copies[2].wait_recv()
        halo[0].wait_recv()
        halo[1].wait_recv()
        image, energy = [], None
        for c in range(2):
            f = field[c]
            upper = jnp.where(xy > 0, halo_in[k, 1, c : c + 1, :], 0.0)
            lower = jnp.where(xy < nx - 1, halo_in[k, 0, c : c + 1, :], 0.0)
            rim = jnp.where(xy > 0, rim_in[...], 0.0)
            gap = f - right[c]
            flux = across * gap
            fall = f - jnp.where(row_id == rows - 1, lower, pltpu.roll(f, rows - 1, 0))
            drop = down * fall
            held = anchor * f
            come = jnp.where(col_id == 0, 0.0, pltpu.roll(flux, 1, 1))
            down_in = jnp.where(row_id == 0, rim * (upper - f), pltpu.roll(drop, 1, 0))
            image.append(flux - come + drop - down_in + held)
            if k == ITERS - 1:
                term = flux * gap + drop * fall + held * f
                energy = term if energy is None else energy + term

        own_copy.wait_recv()
        error_in = [there[c] - point_in[k, 0, c : c + 1, :] for c in range(2)]

        def onward():
            left = unstacked(spread(error_in, mask_left, hot_target, 2), rows, highs)
            more = unstacked(spread(error_in, mask_right, hot_target, 2), rows, highs)
            return [a + pltpu.roll(b, 1, 1) for a, b in zip(left, more)]

        if k < ITERS - 1:
            image = [a + b for a, b in zip(image, onward())]
        there_copy.wait_recv()
        error = [point_in[k, 1, c : c + 1, :] - own[c] for c in range(2)]
        if k == ITERS - 1:
            tie = sum(e * e for e in error)
            last = folded(energy) * (1.0 / SCALE)
            last_tie = folded(tie) * (1.0 / SCALE)
            products.append(last)
            lanes = jnp.concatenate([jnp.sum(p, 0, keepdims=True) for p in products], 0)
            lanes = jnp.concatenate([lanes, jnp.zeros((8 - MOMENTS, 128), jnp.float32)], 0)
            eight = lax.broadcasted_iota(jnp.int32, (8, 128), 0)
            lanes = lanes + jnp.where(eight == MOMENTS - 1, last_tie, 0.0)
            total = jnp.sum(lanes, 1, keepdims=True)
            lane = lax.broadcasted_iota(jnp.int32, (8, 128), 1)
            total = jnp.sum(jnp.where(lane == eight, total, 0.0), 0, keepdims=True)

        def post_sum(stage, total):
            sums[stage, 0] = total
            index = 3 + 4 * ITERS + stage
            for i, peer in enumerate(groups[stage]):
                copy = pltpu.make_async_remote_copy(
                    src_ref=sums.at[stage, 0],
                    dst_ref=sums.at[stage, i + 1],
                    send_sem=send_sem.at[index],
                    recv_sem=recv_sem.at[index],
                    device_id=peer,
                    device_id_type=MESH,
                )
                copy.start()

        def take_sum(stage):
            index = 3 + 4 * ITERS + stage
            count = len(groups[stage])
            arrived = sums.at[stage, pl.ds(1, count)]
            pltpu.make_async_copy(arrived, arrived, recv_sem.at[index]).wait()
            return functools.reduce(lambda a, b: a + b, [sums[stage, i] for i in range(count + 1)])

        if k == ITERS - 1:
            post_sum(0, total)
            image = [a + b for a, b in zip(image, onward())]
        back = unstacked(spread(error, mask_source, hot_source, 2), rows, highs)
        latest = [(a - b) * (1.0 / SCALE) for a, b in zip(image, back)]
        if k < ITERS - 1:
            post_halo(latest, k + 1)
            products.append(sum(folded(a * b) for a, b in zip(field, latest)))
            products.append(sum(folded(a * a) for a in latest))
        for c in range(2):
            basis[k, c] = latest[c]
        field = latest

    for stage in (1, 2):
        total = take_sum(stage - 1)
        post_sum(stage, total)
    total = take_sum(2)
    lane = lax.broadcasted_iota(jnp.int32, (1, 128), 1)
    mu = [
        jnp.sum(jnp.where(lane == i, total, 0.0), 1, keepdims=True) for i in range(MOMENTS)
    ]
    steps, rest = coefficients(mu)
    for c in range(2):
        powers = [rhs_ref[c, 0]] + [basis[i, c] for i in range(ITERS)]
        x_ref[c, 0] = sum((s * (1.0 / SCALE)) * v for s, v in zip(steps, powers))
        r_ref[c, 0] = sum((v if s is None else s * v) for s, v in zip(rest, powers))

    for copy in sent:
        copy.wait_send()
    for stage in range(3):
        count = len(groups[stage])
        gone = sums.at[stage, pl.ds(1, count)]
        pltpu.make_async_copy(gone, gone, send_sem.at[3 + 4 * ITERS + stage]).wait()


def body(nz, rhs, across, down, anchor, source, target, weight, count):
    n_gz, nx = lax.axis_size("gz"), lax.axis_size("xy")
    ny = n_gz // nz
    rows, cols = across.shape[1:]
    slots = source.shape[2]
    places = rows * cols // LOW
    f32, bf16 = jnp.float32, jnp.bfloat16
    vmem = pl.BlockSpec(memory_space=pltpu.VMEM)
    smem = pl.BlockSpec(memory_space=pltpu.SMEM)
    out = jax.ShapeDtypeStruct(rhs.shape, f32)
    copies = 3 + 4 * ITERS + 3
    widest = max(nx, 2 * ny, nz // 2)
    return pl.pallas_call(
        functools.partial(kernel, ny, nz, nx),
        out_shape=(out, out),
        in_specs=[vmem] * 7 + [smem],
        out_specs=(vmem, vmem),
        scratch_shapes=[
            pltpu.VMEM((LOW, slots), bf16),
            pltpu.VMEM((LOW, slots), bf16),
            pltpu.VMEM((places, slots), f32),
            pltpu.VMEM((places, slots), f32),
            pltpu.VMEM((places, slots), f32),
            pltpu.VMEM((ITERS, 2, rows, cols), f32),
            pltpu.VMEM((4, 1, slots), f32),
            pltpu.VMEM((1, cols), f32),
            pltpu.VMEM((ITERS, 2, 2, cols), f32),
            pltpu.VMEM((ITERS, 2, 2, slots), f32),
            pltpu.VMEM((1, 1, slots), jnp.int32),
            pltpu.VMEM((4, 1, slots), f32),
            pltpu.VMEM((1, cols), f32),
            pltpu.VMEM((ITERS, 2, 2, cols), f32),
            pltpu.VMEM((ITERS, 2, 2, slots), f32),
            pltpu.VMEM((3, widest, 1, 128), f32),
            pltpu.SemaphoreType.DMA((copies,)),
            pltpu.SemaphoreType.DMA((copies,)),
        ],
        compiler_params=pltpu.CompilerParams(
            collective_id=0, has_side_effects=True, vmem_limit_bytes=48 * 1024 * 1024
        ),
    )(rhs, across, down, anchor, source, target, weight, count)


def solution(mesh, nz=16):
    in_specs = (
        P(None, "gz", "xy", None),
        P("gz", "xy", None),
        P("gz", "xy", None),
        P("gz", "xy", None),
        P("gz", "xy", None),
        P("gz", "xy", None),
        P(None, "gz", "xy", None),
        P("gz", "xy"),
    )
    out_specs = (P(None, "gz", "xy", None), P(None, "gz", "xy", None))
    return jax.shard_map(
        functools.partial(body, nz), mesh=mesh, in_specs=in_specs, out_specs=out_specs, check_vma=False
    )
```

```python
import functools

import jax
import jax.numpy as jnp
from jax import lax
from jax.experimental import pallas as pl
from jax.experimental.pallas import tpu as pltpu
from jax.sharding import PartitionSpec as P

BLOCK = 128
ITERS = 3
LOW = 256
SCALE = 8.0
MESH = pl.DeviceIdType.MESH
MOMENTS = 2 * ITERS


def pieces(values, count):
    out = []
    for i in range(count):
        part = values.astype(jnp.bfloat16)
        out.append(part)
        if i + 1 < count:
            values = values - part.astype(jnp.float32)
    return jnp.concatenate(out, 0)


def summed(pieces_of, count):
    rows = pieces_of.shape[0] // count
    total = pieces_of[:rows]
    for i in range(1, count):
        total = total + pieces_of[i * rows : (i + 1) * rows]
    return total


def stacked(field):
    return jnp.concatenate(
        [part[:, h : h + LOW] for part in field for h in range(0, part.shape[1], LOW)], 0
    )


def unstacked(table, rows, highs):
    return [
        jnp.concatenate(
            [table[(c * highs + h) * rows : (c * highs + h + 1) * rows] for h in range(highs)], 1
        )
        for c in range(2)
    ]


def looked_up(table, hot, masks, first):
    wide = hot.shape[1]
    cut = min(wide, 256)
    out = []
    for j in range(0, wide, cut):
        found = jnp.dot(table, hot[:, j : j + cut], preferred_element_type=jnp.float32)
        out.append([])
        per = found.shape[0] // len(masks)
        totals = None
        for m, mask in enumerate(masks):
            got = summed(found[m * per : (m + 1) * per], first)
            half = got.shape[0] // 2
            terms = [got[c * half : (c + 1) * half] * mask[:, j : j + cut] for c in range(2)]
            totals = terms if totals is None else [a + b for a, b in zip(totals, terms)]
        out[-1] = [jnp.sum(t, 0, keepdims=True) for t in totals]
    return [jnp.concatenate([o[c] for o in out], 1) for c in range(2)]


def spread(errors, mask, hot, count):
    table = jnp.concatenate([mask[...] * e for e in errors], 0)
    out = lax.dot_general(
        pieces(table, count), hot[...], (((1,), (1,)), ((), ())), preferred_element_type=jnp.float32
    )
    return summed(out, count)


def folded(values):
    return sum(values[:, i : i + 128] for i in range(0, values.shape[1], 128))


def coefficients(mu):
    def inner(a, b, shift):
        total = None
        for i, x in enumerate(a):
            for j, y in enumerate(b):
                term = mu[i + j + shift]
                if x is not None:
                    term = x * term
                if y is not None:
                    term = y * term
                total = term if total is None else total + term
        return total

    residual, direction, field = [None], [None], []
    norm = mu[0]
    for step in range(ITERS):
        alpha = norm / inner(direction, direction, 1)
        along = [alpha if d is None else alpha * d for d in direction]
        field = [a if i >= len(field) else field[i] + a for i, a in enumerate(along)]
        residual = residual[:1] + [
            -a if i + 1 >= len(residual) else residual[i + 1] - a for i, a in enumerate(along)
        ]
        if step + 1 < ITERS:
            fresh = inner(residual, residual, 0)
            ratio = fresh / norm
            step_of = [ratio if d is None else ratio * d for d in direction]
            direction = [
                (1.0 if r is None else r) + (step_of[i] if i < len(step_of) else 0.0)
                for i, r in enumerate(residual)
            ]
            norm = fresh
    return field, residual


def kernel(
    ny,
    nz,
    nx,
    rhs_hbm,
    across_hbm,
    down_hbm,
    anchor_hbm,
    source_hbm,
    target_hbm,
    weight_hbm,
    count_hbm,
    basis,
    scalars,
    rhs_ref,
    across_ref,
    down_ref,
    anchor_ref,
    source_ref,
    weight_ref,
    count_ref,
    hot_source,
    hot_target,
    mask_source,
    mask_left,
    mask_right,
    weight_out,
    rim_out,
    halo_out,
    point_out,
    target_in,
    weight_in,
    rim_in,
    halo_in,
    point_in,
    sums,
    send_sem,
    recv_sem,
    load_sem,
    greet_sem,
):
    rows, cols = across_ref.shape[1:]
    slots = source_ref.shape[2]
    highs = cols // LOW
    bits_cols, bits_low = cols.bit_length() - 1, LOW.bit_length() - 1
    n_gz = ny * nz
    gz, xy = lax.axis_index("gz"), lax.axis_index("xy")
    y, z, x, core = gz // nz, gz % nz, xy // 2, xy % 2
    after, before = ((gz + 1) % n_gz, xy), ((gz + n_gz - 1) % n_gz, xy)
    below, above = (gz, (xy + 1) % nx), (gz, (xy + nx - 1) % nx)

    def peers(offsets):
        sizes = (ny, nz, nx // 2, 2)
        kept = []
        for offset in offsets:
            offset = tuple(o % n for o, n in zip(offset, sizes))
            if any(offset) and offset not in kept:
                kept.append(offset)
        return [
            (((y + o[0]) % ny) * nz + (z + o[1]) % nz, ((x + o[2]) % (nx // 2)) * 2 + (core + o[3]) % 2)
            for o in kept
        ]

    one_hop = peers(
        [(0, 1, 0, 0), (0, -1, 0, 0), (1, 0, 0, 0), (-1, 0, 0, 0), (0, 0, 1, 0), (0, 0, -1, 0), (0, 0, 0, 1)]
    )
    two_hops = peers([(0, 2, 0, 0), (0, -2, 0, 0), (2, 0, 0, 0), (0, 0, 2, 0)])
    four_hops = peers([(0, 4, 0, 0), (0, -4, 0, 0), (0, 0, 0, 1)])
    plane = [(j, 0, i, c) for j in range(ny) for i in range(nx // 2) for c in range(2)]
    line = [(0, i, 0, 0) for i in range(nz)]
    far_first = lambda o: -sum(min(d, n - d) for d, n in zip(o, (ny, nz, nx // 2, 2)))
    groups = [peers(sorted(plane, key=far_first)), peers(sorted(line, key=far_first))]

    barrier = pltpu.get_barrier_semaphore()
    met = [after, before, below, above] + one_hop
    for peer in met:
        pl.semaphore_signal(barrier, inc=1, device_id=peer, device_id_type=MESH)

    def greet(stage, who):
        for peer in who:
            pl.semaphore_signal(greet_sem.at[stage], inc=1, device_id=peer, device_id_type=MESH)

    loads = [
        pltpu.make_async_copy(src, dst, load_sem.at[i])
        for i, (src, dst) in enumerate(
            [
                (count_hbm, count_ref),
                (weight_hbm, weight_ref),
                (source_hbm, source_ref),
                (rhs_hbm, rhs_ref),
                (down_hbm, down_ref),
                (across_hbm, across_ref),
                (anchor_hbm, anchor_ref),
            ]
        )
    ]
    for load in loads:
        load.start()

    sent = []

    def send(src, dst, peer, index):
        copy = pltpu.make_async_remote_copy(
            src_ref=src,
            dst_ref=dst,
            send_sem=send_sem.at[index],
            recv_sem=recv_sem.at[index],
            device_id=peer,
            device_id_type=MESH,
        )
        copy.start()
        sent.append(copy)
        return copy

    slot = lax.broadcasted_iota(jnp.int32, (1, slots), 1)
    loads[0].wait()
    loads[1].wait()
    live = ((slot < count_ref[0, 0] * BLOCK) & (gz < n_gz - 1)).astype(jnp.float32)
    for k in range(4):
        weight_out[k] = weight_ref[k, 0] * live
    def post_halo(field, k):
        for c in range(2):
            halo_out[k, 0, c : c + 1, :] = field[c][:1]
            halo_out[k, 1, c : c + 1, :] = field[c][rows - 1 :]
        return [
            send(halo_out.at[k, 0], halo_in.at[k, 0], above, 3 + 4 * k),
            send(halo_out.at[k, 1], halo_in.at[k, 1], below, 4 + 4 * k),
        ]

    pl.semaphore_wait(barrier, len(met))
    copies = [
        send(target_hbm, target_in, after, 0),
        send(weight_out, weight_in, after, 1),
    ]
    greet(0, one_hop)

    loads[3].wait()
    field = [rhs_ref[c, 0] for c in range(2)]
    halo = post_halo(field, 0)
    loads[4].wait()
    rim_out[...] = down_ref[0, rows - 1 :]
    copies.append(send(rim_out, rim_in, below, 2))

    low_id = lax.broadcasted_iota(jnp.int32, (LOW, slots), 0)
    place_id = lax.broadcasted_iota(jnp.int32, (highs * rows, slots), 0)

    def split(node):
        col = node & (cols - 1)
        return col & (LOW - 1), (col >> bits_low) * rows + (node >> bits_cols)

    loads[2].wait()
    low, place = split(source_ref[0])
    hot_source[...] = (low_id == low).astype(jnp.float32).astype(jnp.bfloat16)
    mask_source[...] = jnp.where(place_id == place, live, 0.0)


    loads[5].wait()
    loads[6].wait()
    across, down, anchor = across_ref[0], down_ref[0], anchor_ref[0]
    col_id = lax.broadcasted_iota(jnp.int32, (rows, cols), 1)
    row_id = lax.broadcasted_iota(jnp.int32, (rows, cols), 0)
    products = [sum(folded(f * f) for f in field)]

    for k in range(ITERS):
        base = 3 + 4 * k
        own = looked_up(pieces(stacked(field), 3), hot_source, [mask_source], 3)
        for c in range(2):
            point_out[k, 0, c : c + 1, :] = own[c]
        own_copy = send(point_out.at[k, 0], point_in.at[k, 0], after, base + 2)
        right = [jnp.where(col_id == cols - 1, 0.0, pltpu.roll(f, cols - 1, 1)) for f in field]
        if k == 0:
            copies[0].wait_recv()
            copies[1].wait_recv()
            low, place = split(target_in[0])
            hot_target[...] = (low_id == low).astype(jnp.float32).astype(jnp.bfloat16)
            for mask, one, two in ((mask_left, 0, 2), (mask_right, 1, 3)):
                mask[...] = jnp.where(
                    place_id == place,
                    weight_in[one],
                    jnp.where(place_id == place + 1, weight_in[two], 0.0),
                )
        table = jnp.concatenate([pieces(stacked(field), 3), pieces(stacked(right), 3)], 0)
        there = looked_up(table, hot_target, [mask_left, mask_right], 3)
        for c in range(2):
            point_out[k, 1, c : c + 1, :] = there[c]
        there_copy = send(point_out.at[k, 1], point_in.at[k, 1], before, base + 3)

        if k == 0:
            copies[2].wait_recv()
        halo[0].wait_recv()
        halo[1].wait_recv()
        image, energy = [], None
        for c in range(2):
            f = field[c]
            upper = jnp.where(xy > 0, halo_in[k, 1, c : c + 1, :], 0.0)
            lower = jnp.where(xy < nx - 1, halo_in[k, 0, c : c + 1, :], 0.0)
            rim = jnp.where(xy > 0, rim_in[...], 0.0)
            gap = f - right[c]
            flux = across * gap
            fall = f - jnp.where(row_id == rows - 1, lower, pltpu.roll(f, rows - 1, 0))
            drop = down * fall
            held = anchor * f
            come = jnp.where(col_id == 0, 0.0, pltpu.roll(flux, 1, 1))
            down_in = jnp.where(row_id == 0, rim * (upper - f), pltpu.roll(drop, 1, 0))
            image.append(flux - come + drop - down_in + held)
            if k == ITERS - 1:
                term = flux * gap + drop * fall + held * f
                energy = term if energy is None else energy + term

        own_copy.wait_recv()
        if k == 0:
            pl.semaphore_wait(greet_sem.at[0], len(one_hop))
            greet(1, two_hops)
        if k == 1:
            pl.semaphore_wait(greet_sem.at[1], len(two_hops))
            greet(2, four_hops)
        error_in = [there[c] - point_in[k, 0, c : c + 1, :] for c in range(2)]

        def onward():
            left = unstacked(spread(error_in, mask_left, hot_target, 2), rows, highs)
            more = unstacked(spread(error_in, mask_right, hot_target, 2), rows, highs)
            return [a + pltpu.roll(b, 1, 1) for a, b in zip(left, more)]

        if k < ITERS - 1:
            image = [a + b for a, b in zip(image, onward())]
        there_copy.wait_recv()
        error = [point_in[k, 1, c : c + 1, :] - own[c] for c in range(2)]
        if k == ITERS - 1:
            tie = sum(e * e for e in error)
            last = folded(energy) * (1.0 / SCALE)
            last_tie = folded(tie) * (1.0 / SCALE)
            products.append(last)
            lanes = jnp.concatenate([jnp.sum(p, 0, keepdims=True) for p in products], 0)
            lanes = jnp.concatenate([lanes, jnp.zeros((8 - MOMENTS, 128), jnp.float32)], 0)
            eight = lax.broadcasted_iota(jnp.int32, (8, 128), 0)
            lanes = lanes + jnp.where(eight == MOMENTS - 1, last_tie, 0.0)
            total = jnp.sum(lanes, 1, keepdims=True)
            lane = lax.broadcasted_iota(jnp.int32, (8, 128), 1)
            total = jnp.sum(jnp.where(lane == eight, total, 0.0), 0, keepdims=True)

        def post_sum(stage, total):
            sums[stage, 0] = total
            if stage == 0:
                pl.semaphore_wait(greet_sem.at[2], len(four_hops))
            index = 3 + 4 * ITERS + stage
            for i, peer in enumerate(groups[stage]):
                copy = pltpu.make_async_remote_copy(
                    src_ref=sums.at[stage, 0],
                    dst_ref=sums.at[stage, i + 1],
                    send_sem=send_sem.at[index],
                    recv_sem=recv_sem.at[index],
                    device_id=peer,
                    device_id_type=MESH,
                )
                copy.start()

        def take_sum(stage):
            index = 3 + 4 * ITERS + stage
            count = len(groups[stage])
            arrived = sums.at[stage, pl.ds(1, count)]
            pltpu.make_async_copy(arrived, arrived, recv_sem.at[index]).wait()
            return functools.reduce(lambda a, b: a + b, [sums[stage, i] for i in range(count + 1)])

        if k == ITERS - 1:
            post_sum(0, total)
            image = [a + b for a, b in zip(image, onward())]
        back = unstacked(spread(error, mask_source, hot_source, 2), rows, highs)
        latest = [(a - b) * (1.0 / SCALE) for a, b in zip(image, back)]
        if k < ITERS - 1:
            halo = post_halo(latest, k + 1)
            products.append(sum(folded(a * b) for a, b in zip(field, latest)))
            products.append(sum(folded(a * a) for a in latest))
        for c in range(2):
            basis[k, c] = latest[c]
        field = latest

    post_sum(1, take_sum(0))
    total = take_sum(1)
    lane = lax.broadcasted_iota(jnp.int32, (1, 128), 1)
    mu = [
        jnp.sum(jnp.where(lane == i, total, 0.0), 1, keepdims=True) for i in range(MOMENTS)
    ]
    steps, rest = coefficients(mu)
    scalars[...] = jnp.concatenate(
        [jnp.broadcast_to(s, (1, 128)) for s in [s * (1.0 / SCALE) for s in steps] + rest[1:]]
        + [jnp.zeros((8 - 2 * ITERS, 128), jnp.float32)],
        0,
    )

    for copy in sent:
        copy.wait_send()
    for stage in range(2):
        count = len(groups[stage])
        gone = sums.at[stage, pl.ds(1, count)]
        pltpu.make_async_copy(gone, gone, send_sem.at[3 + 4 * ITERS + stage]).wait()


def body(nz, rhs, across, down, anchor, source, target, weight, count):
    n_gz, nx = lax.axis_size("gz"), lax.axis_size("xy")
    ny = n_gz // nz
    rows, cols = across.shape[1:]
    slots = source.shape[2]
    places = rows * cols // LOW
    f32, bf16 = jnp.float32, jnp.bfloat16
    vmem = pl.BlockSpec(memory_space=pltpu.VMEM)
    hbm = pl.BlockSpec(memory_space=pltpu.HBM)
    args = (rhs, across, down, anchor, source, target, weight, count)
    copies = 3 + 4 * ITERS + 2
    widest = max(nx * ny, nz)
    basis, scalars = pl.pallas_call(
        functools.partial(kernel, ny, nz, nx),
        out_shape=(
            jax.ShapeDtypeStruct((ITERS, 2, rows, cols), f32),
            jax.ShapeDtypeStruct((8, 128), f32),
        ),
        in_specs=[hbm] * len(args),
        out_specs=(vmem, vmem),
        scratch_shapes=[
            pltpu.VMEM(rhs.shape, f32),
            pltpu.VMEM(across.shape, f32),
            pltpu.VMEM(down.shape, f32),
            pltpu.VMEM(anchor.shape, f32),
            pltpu.VMEM(source.shape, jnp.int32),
            pltpu.VMEM(weight.shape, f32),
            pltpu.SMEM(count.shape, jnp.int32),
            pltpu.VMEM((LOW, slots), bf16),
            pltpu.VMEM((LOW, slots), bf16),
            pltpu.VMEM((places, slots), f32),
            pltpu.VMEM((places, slots), f32),
            pltpu.VMEM((places, slots), f32),
            pltpu.VMEM((4, 1, slots), f32),
            pltpu.VMEM((1, cols), f32),
            pltpu.VMEM((ITERS, 2, 2, cols), f32),
            pltpu.VMEM((ITERS, 2, 2, slots), f32),
            pltpu.VMEM((1, 1, slots), jnp.int32),
            pltpu.VMEM((4, 1, slots), f32),
            pltpu.VMEM((1, cols), f32),
            pltpu.VMEM((ITERS, 2, 2, cols), f32),
            pltpu.VMEM((ITERS, 2, 2, slots), f32),
            pltpu.VMEM((2, widest, 1, 128), f32),
            pltpu.SemaphoreType.DMA((copies,)),
            pltpu.SemaphoreType.DMA((copies,)),
            pltpu.SemaphoreType.DMA((7,)),
            pltpu.SemaphoreType.REGULAR((3,)),
        ],
        compiler_params=pltpu.CompilerParams(
            collective_id=0, has_side_effects=True, vmem_limit_bytes=48 * 1024 * 1024
        ),
    )(*args)
    powers = [rhs[:, 0]] + [basis[i] for i in range(ITERS)]
    field = sum(scalars[i, 0] * powers[i] for i in range(ITERS))
    residual = powers[0] + sum(scalars[ITERS + i, 0] * powers[1 + i] for i in range(ITERS))
    return field[:, None], residual[:, None]


def solution(mesh, nz=16):
    in_specs = (
        P(None, "gz", "xy", None),
        P("gz", "xy", None),
        P("gz", "xy", None),
        P("gz", "xy", None),
        P("gz", "xy", None),
        P("gz", "xy", None),
        P(None, "gz", "xy", None),
        P("gz", "xy"),
    )
    out_specs = (P(None, "gz", "xy", None), P(None, "gz", "xy", None))
    return jax.shard_map(
        functools.partial(body, nz), mesh=mesh, in_specs=in_specs, out_specs=out_specs, check_vma=False
    )
```

```python
import functools

import jax
import jax.numpy as jnp
from jax import lax
from jax.experimental import pallas as pl
from jax.experimental.pallas import tpu as pltpu
from jax.sharding import PartitionSpec as P

BLOCK = 128
ITERS = 3
LOW = 256
SCALE = 8.0
MESH = pl.DeviceIdType.MESH
MOMENTS = 2 * ITERS


def pieces(values, count):
    out = []
    for i in range(count):
        part = values.astype(jnp.bfloat16)
        out.append(part)
        if i + 1 < count:
            values = values - part.astype(jnp.float32)
    return jnp.concatenate(out, 0)


def summed(pieces_of, count):
    rows = pieces_of.shape[0] // count
    total = pieces_of[:rows]
    for i in range(1, count):
        total = total + pieces_of[i * rows : (i + 1) * rows]
    return total


def stacked(field):
    return jnp.concatenate(
        [part[:, h : h + LOW] for part in field for h in range(0, part.shape[1], LOW)], 0
    )


def unstacked(table, rows, highs):
    return [
        jnp.concatenate(
            [table[(c * highs + h) * rows : (c * highs + h + 1) * rows] for h in range(highs)], 1
        )
        for c in range(2)
    ]


def looked_up(table, hot, masks, first):
    wide = hot.shape[1]
    cut = min(wide, 256)
    out = []
    for j in range(0, wide, cut):
        found = jnp.dot(table, hot[:, j : j + cut], preferred_element_type=jnp.float32)
        out.append([])
        per = found.shape[0] // len(masks)
        totals = None
        for m, mask in enumerate(masks):
            got = summed(found[m * per : (m + 1) * per], first)
            half = got.shape[0] // 2
            terms = [got[c * half : (c + 1) * half] * mask[:, j : j + cut] for c in range(2)]
            totals = terms if totals is None else [a + b for a, b in zip(totals, terms)]
        out[-1] = [jnp.sum(t, 0, keepdims=True) for t in totals]
    return [jnp.concatenate([o[c] for o in out], 1) for c in range(2)]


def spread(errors, mask, hot, count):
    table = jnp.concatenate([mask[...] * e for e in errors], 0)
    out = lax.dot_general(
        pieces(table, count), hot[...], (((1,), (1,)), ((), ())), preferred_element_type=jnp.float32
    )
    return summed(out, count)


def folded(values):
    return sum(values[:, i : i + 128] for i in range(0, values.shape[1], 128))


def coefficients(mu):
    def inner(a, b, shift):
        total = None
        for i, x in enumerate(a):
            for j, y in enumerate(b):
                term = mu[i + j + shift]
                if x is not None:
                    term = x * term
                if y is not None:
                    term = y * term
                total = term if total is None else total + term
        return total

    residual, direction, field = [None], [None], []
    norm = mu[0]
    for step in range(ITERS):
        alpha = norm / inner(direction, direction, 1)
        along = [alpha if d is None else alpha * d for d in direction]
        field = [a if i >= len(field) else field[i] + a for i, a in enumerate(along)]
        residual = residual[:1] + [
            -a if i + 1 >= len(residual) else residual[i + 1] - a for i, a in enumerate(along)
        ]
        if step + 1 < ITERS:
            fresh = inner(residual, residual, 0)
            ratio = fresh / norm
            step_of = [ratio if d is None else ratio * d for d in direction]
            direction = [
                (1.0 if r is None else r) + (step_of[i] if i < len(step_of) else 0.0)
                for i, r in enumerate(residual)
            ]
            norm = fresh
    return field, residual


def kernel(
    ny,
    nz,
    nx,
    rhs_hbm,
    across_hbm,
    down_hbm,
    anchor_hbm,
    source_hbm,
    target_hbm,
    weight_hbm,
    count_hbm,
    x_ref,
    r_ref,
    rhs_ref,
    across_ref,
    down_ref,
    anchor_ref,
    source_ref,
    weight_ref,
    count_ref,
    hot_source,
    hot_target,
    mask_source,
    mask_left,
    mask_right,
    basis,
    weight_out,
    rim_out,
    halo_out,
    point_out,
    target_in,
    weight_in,
    rim_in,
    halo_in,
    point_in,
    sums,
    send_sem,
    recv_sem,
    load_sem,
    greet_sem,
):
    rows, cols = across_ref.shape[1:]
    slots = source_ref.shape[2]
    highs = cols // LOW
    bits_cols, bits_low = cols.bit_length() - 1, LOW.bit_length() - 1
    n_gz = ny * nz
    gz, xy = lax.axis_index("gz"), lax.axis_index("xy")
    y, z, x, core = gz // nz, gz % nz, xy // 2, xy % 2
    after, before = ((gz + 1) % n_gz, xy), ((gz + n_gz - 1) % n_gz, xy)
    below, above = (gz, (xy + 1) % nx), (gz, (xy + nx - 1) % nx)

    def peers(offsets):
        sizes = (ny, nz, nx // 2, 2)
        kept = []
        for offset in offsets:
            offset = tuple(o % n for o, n in zip(offset, sizes))
            if any(offset) and offset not in kept:
                kept.append(offset)
        return [
            (((y + o[0]) % ny) * nz + (z + o[1]) % nz, ((x + o[2]) % (nx // 2)) * 2 + (core + o[3]) % 2)
            for o in kept
        ]

    one_hop = peers(
        [(0, 1, 0, 0), (0, -1, 0, 0), (1, 0, 0, 0), (-1, 0, 0, 0), (0, 0, 1, 0), (0, 0, -1, 0), (0, 0, 0, 1)]
    )
    two_hops = peers([(0, 2, 0, 0), (0, -2, 0, 0), (2, 0, 0, 0), (0, 0, 2, 0)])
    four_hops = peers([(0, 4, 0, 0), (0, -4, 0, 0), (0, 0, 0, 1)])
    plane = [(j, 0, i, c) for j in range(ny) for i in range(nx // 2) for c in range(2)]
    line = [(0, i, 0, 0) for i in range(nz)]
    far_first = lambda o: -sum(min(d, n - d) for d, n in zip(o, (ny, nz, nx // 2, 2)))
    groups = [peers(sorted(plane, key=far_first)), peers(sorted(line, key=far_first))]

    barrier = pltpu.get_barrier_semaphore()
    met = [after, before, below, above] + one_hop
    for peer in met:
        pl.semaphore_signal(barrier, inc=1, device_id=peer, device_id_type=MESH)

    def greet(stage, who):
        for peer in who:
            pl.semaphore_signal(greet_sem.at[stage], inc=1, device_id=peer, device_id_type=MESH)

    loads = [
        pltpu.make_async_copy(src, dst, load_sem.at[i])
        for i, (src, dst) in enumerate(
            [
                (count_hbm, count_ref),
                (weight_hbm, weight_ref),
                (source_hbm, source_ref),
                (rhs_hbm, rhs_ref),
                (down_hbm, down_ref),
                (across_hbm, across_ref),
                (anchor_hbm, anchor_ref),
            ]
        )
    ]
    for load in loads:
        load.start()

    sent = []

    def send(src, dst, peer, index):
        copy = pltpu.make_async_remote_copy(
            src_ref=src,
            dst_ref=dst,
            send_sem=send_sem.at[index],
            recv_sem=recv_sem.at[index],
            device_id=peer,
            device_id_type=MESH,
        )
        copy.start()
        sent.append(copy)
        return copy

    slot = lax.broadcasted_iota(jnp.int32, (1, slots), 1)
    loads[0].wait()
    loads[1].wait()
    live = ((slot < count_ref[0, 0] * BLOCK) & (gz < n_gz - 1)).astype(jnp.float32)
    for k in range(4):
        weight_out[k] = weight_ref[k, 0] * live
    def post_halo(field, k):
        for c in range(2):
            halo_out[k, 0, c : c + 1, :] = field[c][:1]
            halo_out[k, 1, c : c + 1, :] = field[c][rows - 1 :]
        return [
            send(halo_out.at[k, 0], halo_in.at[k, 0], above, 3 + 4 * k),
            send(halo_out.at[k, 1], halo_in.at[k, 1], below, 4 + 4 * k),
        ]

    pl.semaphore_wait(barrier, len(met))
    copies = [
        send(target_hbm, target_in, after, 0),
        send(weight_out, weight_in, after, 1),
    ]
    greet(0, one_hop)

    loads[3].wait()
    field = [rhs_ref[c, 0] for c in range(2)]
    halo = post_halo(field, 0)
    loads[4].wait()
    rim_out[...] = down_ref[0, rows - 1 :]
    copies.append(send(rim_out, rim_in, below, 2))

    low_id = lax.broadcasted_iota(jnp.int32, (LOW, slots), 0)
    place_id = lax.broadcasted_iota(jnp.int32, (highs * rows, slots), 0)

    def split(node):
        col = node & (cols - 1)
        return col & (LOW - 1), (col >> bits_low) * rows + (node >> bits_cols)

    loads[2].wait()
    low, place = split(source_ref[0])
    hot_source[...] = (low_id == low).astype(jnp.float32).astype(jnp.bfloat16)
    mask_source[...] = jnp.where(place_id == place, live, 0.0)


    loads[5].wait()
    loads[6].wait()
    across, down, anchor = across_ref[0], down_ref[0], anchor_ref[0]
    col_id = lax.broadcasted_iota(jnp.int32, (rows, cols), 1)
    row_id = lax.broadcasted_iota(jnp.int32, (rows, cols), 0)
    products = [sum(folded(f * f) for f in field)]

    for k in range(ITERS):
        base = 3 + 4 * k
        own = looked_up(pieces(stacked(field), 3), hot_source, [mask_source], 3)
        for c in range(2):
            point_out[k, 0, c : c + 1, :] = own[c]
        own_copy = send(point_out.at[k, 0], point_in.at[k, 0], after, base + 2)
        right = [jnp.where(col_id == cols - 1, 0.0, pltpu.roll(f, cols - 1, 1)) for f in field]
        if k == 0:
            copies[0].wait_recv()
            copies[1].wait_recv()
            low, place = split(target_in[0])
            hot_target[...] = (low_id == low).astype(jnp.float32).astype(jnp.bfloat16)
            for mask, one, two in ((mask_left, 0, 2), (mask_right, 1, 3)):
                mask[...] = jnp.where(
                    place_id == place,
                    weight_in[one],
                    jnp.where(place_id == place + 1, weight_in[two], 0.0),
                )
        table = jnp.concatenate([pieces(stacked(field), 3), pieces(stacked(right), 3)], 0)
        there = looked_up(table, hot_target, [mask_left, mask_right], 3)
        for c in range(2):
            point_out[k, 1, c : c + 1, :] = there[c]
        there_copy = send(point_out.at[k, 1], point_in.at[k, 1], before, base + 3)

        if k == 0:
            copies[2].wait_recv()
        halo[0].wait_recv()
        halo[1].wait_recv()
        image, energy = [], None
        for c in range(2):
            f = field[c]
            upper = jnp.where(xy > 0, halo_in[k, 1, c : c + 1, :], 0.0)
            lower = jnp.where(xy < nx - 1, halo_in[k, 0, c : c + 1, :], 0.0)
            rim = jnp.where(xy > 0, rim_in[...], 0.0)
            gap = f - right[c]
            flux = across * gap
            fall = f - jnp.where(row_id == rows - 1, lower, pltpu.roll(f, rows - 1, 0))
            drop = down * fall
            held = anchor * f
            come = jnp.where(col_id == 0, 0.0, pltpu.roll(flux, 1, 1))
            down_in = jnp.where(row_id == 0, rim * (upper - f), pltpu.roll(drop, 1, 0))
            image.append(flux - come + drop - down_in + held)
            if k == ITERS - 1:
                term = flux * gap + drop * fall + held * f
                energy = term if energy is None else energy + term

        own_copy.wait_recv()
        if k == 0:
            pl.semaphore_wait(greet_sem.at[0], len(one_hop))
            greet(1, two_hops)
        if k == 1:
            pl.semaphore_wait(greet_sem.at[1], len(two_hops))
            greet(2, four_hops)
        error_in = [there[c] - point_in[k, 0, c : c + 1, :] for c in range(2)]

        def onward():
            left = unstacked(spread(error_in, mask_left, hot_target, 2), rows, highs)
            more = unstacked(spread(error_in, mask_right, hot_target, 2), rows, highs)
            return [a + pltpu.roll(b, 1, 1) for a, b in zip(left, more)]

        if k < ITERS - 1:
            image = [a + b for a, b in zip(image, onward())]
        there_copy.wait_recv()
        error = [point_in[k, 1, c : c + 1, :] - own[c] for c in range(2)]
        if k == ITERS - 1:
            tie = sum(e * e for e in error)
            last = folded(energy) * (1.0 / SCALE)
            last_tie = folded(tie) * (1.0 / SCALE)
            products.append(last)
            lanes = jnp.concatenate([jnp.sum(p, 0, keepdims=True) for p in products], 0)
            lanes = jnp.concatenate([lanes, jnp.zeros((8 - MOMENTS, 128), jnp.float32)], 0)
            eight = lax.broadcasted_iota(jnp.int32, (8, 128), 0)
            lanes = lanes + jnp.where(eight == MOMENTS - 1, last_tie, 0.0)
            total = jnp.sum(lanes, 1, keepdims=True)
            lane = lax.broadcasted_iota(jnp.int32, (8, 128), 1)
            total = jnp.sum(jnp.where(lane == eight, total, 0.0), 0, keepdims=True)

        def post_sum(stage, total):
            sums[stage, 0] = total
            if stage == 0:
                pl.semaphore_wait(greet_sem.at[2], len(four_hops))
            index = 3 + 4 * ITERS + stage
            for i, peer in enumerate(groups[stage]):
                copy = pltpu.make_async_remote_copy(
                    src_ref=sums.at[stage, 0],
                    dst_ref=sums.at[stage, i + 1],
                    send_sem=send_sem.at[index],
                    recv_sem=recv_sem.at[index],
                    device_id=peer,
                    device_id_type=MESH,
                )
                copy.start()

        def take_sum(stage):
            index = 3 + 4 * ITERS + stage
            count = len(groups[stage])
            arrived = sums.at[stage, pl.ds(1, count)]
            pltpu.make_async_copy(arrived, arrived, recv_sem.at[index]).wait()
            return functools.reduce(lambda a, b: a + b, [sums[stage, i] for i in range(count + 1)])

        if k == ITERS - 1:
            post_sum(0, total)
            image = [a + b for a, b in zip(image, onward())]
        back = unstacked(spread(error, mask_source, hot_source, 2), rows, highs)
        latest = [(a - b) * (1.0 / SCALE) for a, b in zip(image, back)]
        if k < ITERS - 1:
            halo = post_halo(latest, k + 1)
            products.append(sum(folded(a * b) for a, b in zip(field, latest)))
            products.append(sum(folded(a * a) for a in latest))
        for c in range(2):
            basis[k, c] = latest[c]
        field = latest

    post_sum(1, take_sum(0))
    total = take_sum(1)
    lane = lax.broadcasted_iota(jnp.int32, (1, 128), 1)
    mu = [
        jnp.sum(jnp.where(lane == i, total, 0.0), 1, keepdims=True) for i in range(MOMENTS)
    ]
    steps, rest = coefficients(mu)
    for c in range(2):
        powers = [rhs_ref[c, 0]] + [basis[i, c] for i in range(ITERS)]
        x_ref[c, 0] = sum((s * (1.0 / SCALE)) * v for s, v in zip(steps, powers))
        r_ref[c, 0] = sum((v if s is None else s * v) for s, v in zip(rest, powers))

    for copy in sent:
        copy.wait_send()
    for stage in range(2):
        count = len(groups[stage])
        gone = sums.at[stage, pl.ds(1, count)]
        pltpu.make_async_copy(gone, gone, send_sem.at[3 + 4 * ITERS + stage]).wait()


def body(nz, rhs, across, down, anchor, source, target, weight, count):
    n_gz, nx = lax.axis_size("gz"), lax.axis_size("xy")
    ny = n_gz // nz
    rows, cols = across.shape[1:]
    slots = source.shape[2]
    places = rows * cols // LOW
    f32, bf16 = jnp.float32, jnp.bfloat16
    vmem = pl.BlockSpec(memory_space=pltpu.VMEM)
    hbm = pl.BlockSpec(memory_space=pltpu.HBM)
    args = (rhs, across, down, anchor, source, target, weight, count)
    copies = 3 + 4 * ITERS + 2
    widest = max(nx * ny, nz)
    out = jax.ShapeDtypeStruct(rhs.shape, f32)
    return pl.pallas_call(
        functools.partial(kernel, ny, nz, nx),
        out_shape=(out, out),
        in_specs=[hbm] * len(args),
        out_specs=(vmem, vmem),
        scratch_shapes=[
            pltpu.VMEM(rhs.shape, f32),
            pltpu.VMEM(across.shape, f32),
            pltpu.VMEM(down.shape, f32),
            pltpu.VMEM(anchor.shape, f32),
            pltpu.VMEM(source.shape, jnp.int32),
            pltpu.VMEM(weight.shape, f32),
            pltpu.SMEM(count.shape, jnp.int32),
            pltpu.VMEM((LOW, slots), bf16),
            pltpu.VMEM((LOW, slots), bf16),
            pltpu.VMEM((places, slots), f32),
            pltpu.VMEM((places, slots), f32),
            pltpu.VMEM((places, slots), f32),
            pltpu.VMEM((ITERS, 2, rows, cols), f32),
            pltpu.VMEM((4, 1, slots), f32),
            pltpu.VMEM((1, cols), f32),
            pltpu.VMEM((ITERS, 2, 2, cols), f32),
            pltpu.VMEM((ITERS, 2, 2, slots), f32),
            pltpu.VMEM((1, 1, slots), jnp.int32),
            pltpu.VMEM((4, 1, slots), f32),
            pltpu.VMEM((1, cols), f32),
            pltpu.VMEM((ITERS, 2, 2, cols), f32),
            pltpu.VMEM((ITERS, 2, 2, slots), f32),
            pltpu.VMEM((2, widest, 1, 128), f32),
            pltpu.SemaphoreType.DMA((copies,)),
            pltpu.SemaphoreType.DMA((copies,)),
            pltpu.SemaphoreType.DMA((7,)),
            pltpu.SemaphoreType.REGULAR((3,)),
        ],
        compiler_params=pltpu.CompilerParams(
            collective_id=0, has_side_effects=True, vmem_limit_bytes=63 * 1024 * 1024
        ),
    )(*args)


def solution(mesh, nz=16):
    in_specs = (
        P(None, "gz", "xy", None),
        P("gz", "xy", None),
        P("gz", "xy", None),
        P("gz", "xy", None),
        P("gz", "xy", None),
        P("gz", "xy", None),
        P(None, "gz", "xy", None),
        P("gz", "xy"),
    )
    out_specs = (P(None, "gz", "xy", None), P(None, "gz", "xy", None))
    return jax.shard_map(
        functools.partial(body, nz), mesh=mesh, in_specs=in_specs, out_specs=out_specs, check_vma=False
    )
```

```python
import functools

import jax
import jax.numpy as jnp
from jax import lax
from jax.experimental import pallas as pl
from jax.experimental.pallas import tpu as pltpu
from jax.sharding import PartitionSpec as P

BLOCK = 128
ITERS = 3
LOW = 256
SCALE = 8.0
MESH = pl.DeviceIdType.MESH
MOMENTS = 2 * ITERS


def pieces(values, count):
    out = []
    for i in range(count):
        part = values.astype(jnp.bfloat16)
        out.append(part)
        if i + 1 < count:
            values = values - part.astype(jnp.float32)
    return jnp.concatenate(out, 0)


def summed(pieces_of, count):
    rows = pieces_of.shape[0] // count
    total = pieces_of[:rows]
    for i in range(1, count):
        total = total + pieces_of[i * rows : (i + 1) * rows]
    return total


def stacked(field):
    return jnp.concatenate(
        [part[:, h : h + LOW] for part in field for h in range(0, part.shape[1], LOW)], 0
    )


def unstacked(table, rows, highs):
    return [
        jnp.concatenate(
            [table[(c * highs + h) * rows : (c * highs + h + 1) * rows] for h in range(highs)], 1
        )
        for c in range(2)
    ]


def looked_up(table, hot, masks, first):
    wide = hot.shape[1]
    cut = min(wide, 256)
    out = []
    for j in range(0, wide, cut):
        found = jnp.dot(table, hot[:, j : j + cut], preferred_element_type=jnp.float32)
        out.append([])
        per = found.shape[0] // len(masks)
        totals = None
        for m, mask in enumerate(masks):
            got = summed(found[m * per : (m + 1) * per], first)
            half = got.shape[0] // 2
            terms = [got[c * half : (c + 1) * half] * mask[:, j : j + cut] for c in range(2)]
            totals = terms if totals is None else [a + b for a, b in zip(totals, terms)]
        out[-1] = [jnp.sum(t, 0, keepdims=True) for t in totals]
    return [jnp.concatenate([o[c] for o in out], 1) for c in range(2)]


def spread(errors, mask, hot, count):
    table = jnp.concatenate([mask[...] * e for e in errors], 0)
    out = lax.dot_general(
        pieces(table, count), hot[...], (((1,), (1,)), ((), ())), preferred_element_type=jnp.float32
    )
    return summed(out, count)


def folded(values):
    return sum(values[:, i : i + 128] for i in range(0, values.shape[1], 128))


def coefficients(mu):
    def inner(a, b, shift):
        total = None
        for i, x in enumerate(a):
            for j, y in enumerate(b):
                term = mu[i + j + shift]
                if x is not None:
                    term = x * term
                if y is not None:
                    term = y * term
                total = term if total is None else total + term
        return total

    residual, direction, field = [None], [None], []
    norm = mu[0]
    for step in range(ITERS):
        alpha = norm / inner(direction, direction, 1)
        along = [alpha if d is None else alpha * d for d in direction]
        field = [a if i >= len(field) else field[i] + a for i, a in enumerate(along)]
        residual = residual[:1] + [
            -a if i + 1 >= len(residual) else residual[i + 1] - a for i, a in enumerate(along)
        ]
        if step + 1 < ITERS:
            fresh = inner(residual, residual, 0)
            ratio = fresh / norm
            step_of = [ratio if d is None else ratio * d for d in direction]
            direction = [
                (1.0 if r is None else r) + (step_of[i] if i < len(step_of) else 0.0)
                for i, r in enumerate(residual)
            ]
            norm = fresh
    return field, residual


def kernel(
    ny,
    nz,
    nx,
    rhs_hbm,
    across_hbm,
    down_hbm,
    anchor_hbm,
    source_hbm,
    target_hbm,
    weight_hbm,
    count_hbm,
    basis_hbm,
    scalars,
    rhs_ref,
    across_ref,
    down_ref,
    anchor_ref,
    source_ref,
    weight_ref,
    count_ref,
    hot_source,
    hot_target,
    mask_source,
    mask_left,
    mask_right,
    basis,
    weight_out,
    rim_out,
    halo_out,
    point_out,
    target_in,
    weight_in,
    rim_in,
    halo_in,
    point_in,
    sums,
    send_sem,
    recv_sem,
    load_sem,
    keep_sem,
    greet_sem,
):
    rows, cols = across_ref.shape[1:]
    slots = source_ref.shape[2]
    highs = cols // LOW
    bits_cols, bits_low = cols.bit_length() - 1, LOW.bit_length() - 1
    n_gz = ny * nz
    gz, xy = lax.axis_index("gz"), lax.axis_index("xy")
    y, z, x, core = gz // nz, gz % nz, xy // 2, xy % 2
    after, before = ((gz + 1) % n_gz, xy), ((gz + n_gz - 1) % n_gz, xy)
    below, above = (gz, (xy + 1) % nx), (gz, (xy + nx - 1) % nx)

    def peers(offsets):
        sizes = (ny, nz, nx // 2, 2)
        kept = []
        for offset in offsets:
            offset = tuple(o % n for o, n in zip(offset, sizes))
            if any(offset) and offset not in kept:
                kept.append(offset)
        return [
            (((y + o[0]) % ny) * nz + (z + o[1]) % nz, ((x + o[2]) % (nx // 2)) * 2 + (core + o[3]) % 2)
            for o in kept
        ]

    one_hop = peers(
        [(0, 1, 0, 0), (0, -1, 0, 0), (1, 0, 0, 0), (-1, 0, 0, 0), (0, 0, 1, 0), (0, 0, -1, 0), (0, 0, 0, 1)]
    )
    two_hops = peers([(0, 2, 0, 0), (0, -2, 0, 0), (2, 0, 0, 0), (0, 0, 2, 0)])
    four_hops = peers([(0, 4, 0, 0), (0, -4, 0, 0), (0, 0, 0, 1)])
    plane = [(j, 0, i, c) for j in range(ny) for i in range(nx // 2) for c in range(2)]
    line = [(0, i, 0, 0) for i in range(nz)]
    far_first = lambda o: -sum(min(d, n - d) for d, n in zip(o, (ny, nz, nx // 2, 2)))
    groups = [peers(sorted(plane, key=far_first)), peers(sorted(line, key=far_first))]

    barrier = pltpu.get_barrier_semaphore()
    met = [after, before, below, above] + one_hop
    for peer in met:
        pl.semaphore_signal(barrier, inc=1, device_id=peer, device_id_type=MESH)

    def greet(stage, who):
        for peer in who:
            pl.semaphore_signal(greet_sem.at[stage], inc=1, device_id=peer, device_id_type=MESH)

    loads = [
        pltpu.make_async_copy(src, dst, load_sem.at[i])
        for i, (src, dst) in enumerate(
            [
                (count_hbm, count_ref),
                (weight_hbm, weight_ref),
                (source_hbm, source_ref),
                (rhs_hbm, rhs_ref),
                (down_hbm, down_ref),
                (across_hbm, across_ref),
                (anchor_hbm, anchor_ref),
            ]
        )
    ]
    for load in loads:
        load.start()

    sent, kept = [], []

    def send(src, dst, peer, index):
        copy = pltpu.make_async_remote_copy(
            src_ref=src,
            dst_ref=dst,
            send_sem=send_sem.at[index],
            recv_sem=recv_sem.at[index],
            device_id=peer,
            device_id_type=MESH,
        )
        copy.start()
        sent.append(copy)
        return copy

    slot = lax.broadcasted_iota(jnp.int32, (1, slots), 1)
    loads[0].wait()
    loads[1].wait()
    live = ((slot < count_ref[0, 0] * BLOCK) & (gz < n_gz - 1)).astype(jnp.float32)
    for k in range(4):
        weight_out[k] = weight_ref[k, 0] * live
    def post_halo(field, k):
        for c in range(2):
            halo_out[k, 0, c : c + 1, :] = field[c][:1]
            halo_out[k, 1, c : c + 1, :] = field[c][rows - 1 :]
        return [
            send(halo_out.at[k, 0], halo_in.at[k, 0], above, 3 + 4 * k),
            send(halo_out.at[k, 1], halo_in.at[k, 1], below, 4 + 4 * k),
        ]

    pl.semaphore_wait(barrier, len(met))
    copies = [
        send(target_hbm, target_in, after, 0),
        send(weight_out, weight_in, after, 1),
    ]
    greet(0, one_hop)

    loads[3].wait()
    field = [rhs_ref[c, 0] for c in range(2)]
    halo = post_halo(field, 0)
    loads[4].wait()
    rim_out[...] = down_ref[0, rows - 1 :]
    copies.append(send(rim_out, rim_in, below, 2))

    low_id = lax.broadcasted_iota(jnp.int32, (LOW, slots), 0)
    place_id = lax.broadcasted_iota(jnp.int32, (highs * rows, slots), 0)

    def split(node):
        col = node & (cols - 1)
        return col & (LOW - 1), (col >> bits_low) * rows + (node >> bits_cols)

    loads[2].wait()
    low, place = split(source_ref[0])
    hot_source[...] = (low_id == low).astype(jnp.float32).astype(jnp.bfloat16)
    mask_source[...] = jnp.where(place_id == place, live, 0.0)


    loads[5].wait()
    loads[6].wait()
    across, down, anchor = across_ref[0], down_ref[0], anchor_ref[0]
    col_id = lax.broadcasted_iota(jnp.int32, (rows, cols), 1)
    row_id = lax.broadcasted_iota(jnp.int32, (rows, cols), 0)
    products = [sum(folded(f * f) for f in field)]

    for k in range(ITERS):
        base = 3 + 4 * k
        own = looked_up(pieces(stacked(field), 3), hot_source, [mask_source], 3)
        for c in range(2):
            point_out[k, 0, c : c + 1, :] = own[c]
        own_copy = send(point_out.at[k, 0], point_in.at[k, 0], after, base + 2)
        right = [jnp.where(col_id == cols - 1, 0.0, pltpu.roll(f, cols - 1, 1)) for f in field]
        if k == 0:
            copies[0].wait_recv()
            copies[1].wait_recv()
            low, place = split(target_in[0])
            hot_target[...] = (low_id == low).astype(jnp.float32).astype(jnp.bfloat16)
            for mask, one, two in ((mask_left, 0, 2), (mask_right, 1, 3)):
                mask[...] = jnp.where(
                    place_id == place,
                    weight_in[one],
                    jnp.where(place_id == place + 1, weight_in[two], 0.0),
                )
        table = jnp.concatenate([pieces(stacked(field), 3), pieces(stacked(right), 3)], 0)
        there = looked_up(table, hot_target, [mask_left, mask_right], 3)
        for c in range(2):
            point_out[k, 1, c : c + 1, :] = there[c]
        there_copy = send(point_out.at[k, 1], point_in.at[k, 1], before, base + 3)

        if k == 0:
            copies[2].wait_recv()
        halo[0].wait_recv()
        halo[1].wait_recv()
        image, energy = [], None
        for c in range(2):
            f = field[c]
            upper = jnp.where(xy > 0, halo_in[k, 1, c : c + 1, :], 0.0)
            lower = jnp.where(xy < nx - 1, halo_in[k, 0, c : c + 1, :], 0.0)
            rim = jnp.where(xy > 0, rim_in[...], 0.0)
            gap = f - right[c]
            flux = across * gap
            fall = f - jnp.where(row_id == rows - 1, lower, pltpu.roll(f, rows - 1, 0))
            drop = down * fall
            held = anchor * f
            come = jnp.where(col_id == 0, 0.0, pltpu.roll(flux, 1, 1))
            down_in = jnp.where(row_id == 0, rim * (upper - f), pltpu.roll(drop, 1, 0))
            image.append(flux - come + drop - down_in + held)
            if k == ITERS - 1:
                term = flux * gap + drop * fall + held * f
                energy = term if energy is None else energy + term

        own_copy.wait_recv()
        if k == 0:
            pl.semaphore_wait(greet_sem.at[0], len(one_hop))
            greet(1, two_hops)
        if k == 1:
            pl.semaphore_wait(greet_sem.at[1], len(two_hops))
            greet(2, four_hops)
        error_in = [there[c] - point_in[k, 0, c : c + 1, :] for c in range(2)]

        def onward():
            left = unstacked(spread(error_in, mask_left, hot_target, 2), rows, highs)
            more = unstacked(spread(error_in, mask_right, hot_target, 2), rows, highs)
            return [a + pltpu.roll(b, 1, 1) for a, b in zip(left, more)]

        if k < ITERS - 1:
            image = [a + b for a, b in zip(image, onward())]
        there_copy.wait_recv()
        error = [point_in[k, 1, c : c + 1, :] - own[c] for c in range(2)]
        if k == ITERS - 1:
            tie = sum(e * e for e in error)
            last = folded(energy) * (1.0 / SCALE)
            last_tie = folded(tie) * (1.0 / SCALE)
            products.append(last)
            lanes = jnp.concatenate([jnp.sum(p, 0, keepdims=True) for p in products], 0)
            lanes = jnp.concatenate([lanes, jnp.zeros((8 - MOMENTS, 128), jnp.float32)], 0)
            eight = lax.broadcasted_iota(jnp.int32, (8, 128), 0)
            lanes = lanes + jnp.where(eight == MOMENTS - 1, last_tie, 0.0)
            total = jnp.sum(lanes, 1, keepdims=True)
            lane = lax.broadcasted_iota(jnp.int32, (8, 128), 1)
            total = jnp.sum(jnp.where(lane == eight, total, 0.0), 0, keepdims=True)

        def post_sum(stage, total):
            sums[stage, 0] = total
            if stage == 0:
                pl.semaphore_wait(greet_sem.at[2], len(four_hops))
            index = 3 + 4 * ITERS + stage
            for i, peer in enumerate(groups[stage]):
                copy = pltpu.make_async_remote_copy(
                    src_ref=sums.at[stage, 0],
                    dst_ref=sums.at[stage, i + 1],
                    send_sem=send_sem.at[index],
                    recv_sem=recv_sem.at[index],
                    device_id=peer,
                    device_id_type=MESH,
                )
                copy.start()

        def take_sum(stage):
            index = 3 + 4 * ITERS + stage
            count = len(groups[stage])
            arrived = sums.at[stage, pl.ds(1, count)]
            pltpu.make_async_copy(arrived, arrived, recv_sem.at[index]).wait()
            return functools.reduce(lambda a, b: a + b, [sums[stage, i] for i in range(count + 1)])

        if k == ITERS - 1:
            post_sum(0, total)
            image = [a + b for a, b in zip(image, onward())]
        back = unstacked(spread(error, mask_source, hot_source, 2), rows, highs)
        latest = [(a - b) * (1.0 / SCALE) for a, b in zip(image, back)]
        if k < ITERS - 1:
            halo = post_halo(latest, k + 1)
            products.append(sum(folded(a * b) for a, b in zip(field, latest)))
            products.append(sum(folded(a * a) for a in latest))
        for c in range(2):
            basis[k, c] = latest[c]
        keep = pltpu.make_async_copy(basis.at[k], basis_hbm.at[k], keep_sem.at[k])
        keep.start()
        kept.append(keep)
        field = latest

    post_sum(1, take_sum(0))
    total = take_sum(1)
    lane = lax.broadcasted_iota(jnp.int32, (1, 128), 1)
    mu = [
        jnp.sum(jnp.where(lane == i, total, 0.0), 1, keepdims=True) for i in range(MOMENTS)
    ]
    steps, rest = coefficients(mu)
    rows_of = [jnp.broadcast_to(s, (1, 128)) for s in [s * (1.0 / SCALE) for s in steps] + rest[1:]]
    scalars[...] = jnp.concatenate(rows_of + [jnp.zeros((8 - 2 * ITERS, 128), jnp.float32)], 0)

    for keep in kept:
        keep.wait()
    for copy in sent:
        copy.wait_send()
    for stage in range(2):
        count = len(groups[stage])
        gone = sums.at[stage, pl.ds(1, count)]
        pltpu.make_async_copy(gone, gone, send_sem.at[3 + 4 * ITERS + stage]).wait()


def combine(rhs_hbm, basis_hbm, scalars_hbm, x_hbm, r_hbm, rhs, basis, scalars, x, r, load_sem, save_sem):
    loads = [
        pltpu.make_async_copy(src, dst, load_sem.at[i])
        for i, (src, dst) in enumerate(((scalars_hbm, scalars), (rhs_hbm, rhs), (basis_hbm, basis)))
    ]
    for load in loads:
        load.start()
    for load in loads:
        load.wait()
    values = [scalars[i : i + 1, :1] for i in range(2 * ITERS)]
    saves = []
    for c in range(2):
        powers = [rhs[c, 0]] + [basis[i, c] for i in range(ITERS)]
        x[c, 0] = sum(s * v for s, v in zip(values[:ITERS], powers))
        r[c, 0] = powers[0] + sum(s * v for s, v in zip(values[ITERS:], powers[1:]))
        for n, (src, dst) in enumerate(((x, x_hbm), (r, r_hbm))):
            save = pltpu.make_async_copy(src.at[c], dst.at[c], save_sem.at[2 * c + n])
            save.start()
            saves.append(save)
    for save in saves:
        save.wait()


def body(nz, rhs, across, down, anchor, source, target, weight, count):
    n_gz, nx = lax.axis_size("gz"), lax.axis_size("xy")
    ny = n_gz // nz
    rows, cols = across.shape[1:]
    slots = source.shape[2]
    places = rows * cols // LOW
    f32, bf16 = jnp.float32, jnp.bfloat16
    vmem = pl.BlockSpec(memory_space=pltpu.VMEM)
    hbm = pl.BlockSpec(memory_space=pltpu.HBM)
    args = (rhs, across, down, anchor, source, target, weight, count)
    copies = 3 + 4 * ITERS + 2
    widest = max(nx * ny, nz)
    basis, scalars = pl.pallas_call(
        functools.partial(kernel, ny, nz, nx),
        out_shape=(
            jax.ShapeDtypeStruct((ITERS, 2, rows, cols), f32),
            jax.ShapeDtypeStruct((8, 128), f32),
        ),
        in_specs=[hbm] * len(args),
        out_specs=(hbm, vmem),
        scratch_shapes=[
            pltpu.VMEM(rhs.shape, f32),
            pltpu.VMEM(across.shape, f32),
            pltpu.VMEM(down.shape, f32),
            pltpu.VMEM(anchor.shape, f32),
            pltpu.VMEM(source.shape, jnp.int32),
            pltpu.VMEM(weight.shape, f32),
            pltpu.SMEM(count.shape, jnp.int32),
            pltpu.VMEM((LOW, slots), bf16),
            pltpu.VMEM((LOW, slots), bf16),
            pltpu.VMEM((places, slots), f32),
            pltpu.VMEM((places, slots), f32),
            pltpu.VMEM((places, slots), f32),
            pltpu.VMEM((ITERS, 2, rows, cols), f32),
            pltpu.VMEM((4, 1, slots), f32),
            pltpu.VMEM((1, cols), f32),
            pltpu.VMEM((ITERS, 2, 2, cols), f32),
            pltpu.VMEM((ITERS, 2, 2, slots), f32),
            pltpu.VMEM((1, 1, slots), jnp.int32),
            pltpu.VMEM((4, 1, slots), f32),
            pltpu.VMEM((1, cols), f32),
            pltpu.VMEM((ITERS, 2, 2, cols), f32),
            pltpu.VMEM((ITERS, 2, 2, slots), f32),
            pltpu.VMEM((2, widest, 1, 128), f32),
            pltpu.SemaphoreType.DMA((copies,)),
            pltpu.SemaphoreType.DMA((copies,)),
            pltpu.SemaphoreType.DMA((7,)),
            pltpu.SemaphoreType.DMA((ITERS,)),
            pltpu.SemaphoreType.REGULAR((3,)),
        ],
        compiler_params=pltpu.CompilerParams(
            collective_id=0, has_side_effects=True, vmem_limit_bytes=63 * 1024 * 1024
        ),
    )(*args)
    out = jax.ShapeDtypeStruct(rhs.shape, f32)
    return pl.pallas_call(
        combine,
        out_shape=(out, out),
        in_specs=[hbm] * 3,
        out_specs=(hbm, hbm),
        scratch_shapes=[
            pltpu.VMEM(rhs.shape, f32),
            pltpu.VMEM(basis.shape, f32),
            pltpu.VMEM(scalars.shape, f32),
            pltpu.VMEM(rhs.shape, f32),
            pltpu.VMEM(rhs.shape, f32),
            pltpu.SemaphoreType.DMA((3,)),
            pltpu.SemaphoreType.DMA((4,)),
        ],
        compiler_params=pltpu.CompilerParams(vmem_limit_bytes=63 * 1024 * 1024),
    )(rhs, basis, scalars)


def solution(mesh, nz=16):
    in_specs = (
        P(None, "gz", "xy", None),
        P("gz", "xy", None),
        P("gz", "xy", None),
        P("gz", "xy", None),
        P("gz", "xy", None),
        P("gz", "xy", None),
        P(None, "gz", "xy", None),
        P("gz", "xy"),
    )
    out_specs = (P(None, "gz", "xy", None), P(None, "gz", "xy", None))
    return jax.shard_map(
        functools.partial(body, nz), mesh=mesh, in_specs=in_specs, out_specs=out_specs, check_vma=False
    )
```

```python
import functools

import jax
import jax.numpy as jnp
from jax import lax
from jax.experimental import pallas as pl
from jax.experimental.pallas import tpu as pltpu
from jax.sharding import PartitionSpec as P

BLOCK = 128
ITERS = 3
LOW = 256
SCALE = 8.0
MESH = pl.DeviceIdType.MESH
MOMENTS = 2 * ITERS


def pieces(values, count):
    out = []
    for i in range(count):
        part = values.astype(jnp.bfloat16)
        out.append(part)
        if i + 1 < count:
            values = values - part.astype(jnp.float32)
    return jnp.concatenate(out, 0)


def summed(pieces_of, count):
    rows = pieces_of.shape[0] // count
    total = pieces_of[:rows]
    for i in range(1, count):
        total = total + pieces_of[i * rows : (i + 1) * rows]
    return total


def stacked(field):
    return jnp.concatenate(
        [part[:, h : h + LOW] for part in field for h in range(0, part.shape[1], LOW)], 0
    )


def unstacked(table, rows, highs):
    return [
        jnp.concatenate(
            [table[(c * highs + h) * rows : (c * highs + h + 1) * rows] for h in range(highs)], 1
        )
        for c in range(2)
    ]


def looked_up(table, hot, masks, first):
    wide = hot.shape[1]
    cut = min(wide, 256)
    out = []
    for j in range(0, wide, cut):
        found = jnp.dot(table, hot[:, j : j + cut], preferred_element_type=jnp.float32)
        out.append([])
        per = found.shape[0] // len(masks)
        totals = None
        for m, mask in enumerate(masks):
            got = summed(found[m * per : (m + 1) * per], first)
            half = got.shape[0] // 2
            terms = [got[c * half : (c + 1) * half] * mask[:, j : j + cut] for c in range(2)]
            totals = terms if totals is None else [a + b for a, b in zip(totals, terms)]
        out[-1] = [jnp.sum(t, 0, keepdims=True) for t in totals]
    return [jnp.concatenate([o[c] for o in out], 1) for c in range(2)]


def spread(errors, mask, hot, count):
    table = jnp.concatenate([mask[...] * e for e in errors], 0)
    out = lax.dot_general(
        pieces(table, count), hot[...], (((1,), (1,)), ((), ())), preferred_element_type=jnp.float32
    )
    return summed(out, count)


def folded(values):
    return sum(values[:, i : i + 128] for i in range(0, values.shape[1], 128))


def coefficients(mu):
    def inner(a, b, shift):
        total = None
        for i, x in enumerate(a):
            for j, y in enumerate(b):
                term = mu[i + j + shift]
                if x is not None:
                    term = x * term
                if y is not None:
                    term = y * term
                total = term if total is None else total + term
        return total

    residual, direction, field = [None], [None], []
    norm = mu[0]
    for step in range(ITERS):
        alpha = norm / inner(direction, direction, 1)
        along = [alpha if d is None else alpha * d for d in direction]
        field = [a if i >= len(field) else field[i] + a for i, a in enumerate(along)]
        residual = residual[:1] + [
            -a if i + 1 >= len(residual) else residual[i + 1] - a for i, a in enumerate(along)
        ]
        if step + 1 < ITERS:
            fresh = inner(residual, residual, 0)
            ratio = fresh / norm
            step_of = [ratio if d is None else ratio * d for d in direction]
            direction = [
                (1.0 if r is None else r) + (step_of[i] if i < len(step_of) else 0.0)
                for i, r in enumerate(residual)
            ]
            norm = fresh
    return field, residual


def kernel(
    ny,
    nz,
    nx,
    rhs_hbm,
    across_hbm,
    down_hbm,
    anchor_hbm,
    source_hbm,
    target_hbm,
    weight_hbm,
    count_hbm,
    basis_hbm,
    scalars,
    rhs_ref,
    across_ref,
    down_ref,
    anchor_ref,
    source_ref,
    target_ref,
    weight_ref,
    count_ref,
    hot_source,
    hot_target,
    mask_source,
    mask_left,
    mask_right,
    basis,
    slot_out,
    rim_out,
    halo_out,
    point_out,
    slot_in,
    rim_in,
    halo_in,
    point_in,
    sums,
    send_sem,
    recv_sem,
    load_sem,
    keep_sem,
    greet_sem,
):
    rows, cols = across_ref.shape[1:]
    slots = source_ref.shape[2]
    highs = cols // LOW
    bits_cols, bits_low = cols.bit_length() - 1, LOW.bit_length() - 1
    n_gz = ny * nz
    gz, xy = lax.axis_index("gz"), lax.axis_index("xy")
    y, z, x, core = gz // nz, gz % nz, xy // 2, xy % 2
    after, before = ((gz + 1) % n_gz, xy), ((gz + n_gz - 1) % n_gz, xy)
    below, above = (gz, (xy + 1) % nx), (gz, (xy + nx - 1) % nx)

    def peers(offsets):
        sizes = (ny, nz, nx // 2, 2)
        kept = []
        for offset in offsets:
            offset = tuple(o % n for o, n in zip(offset, sizes))
            if any(offset) and offset not in kept:
                kept.append(offset)
        return [
            (((y + o[0]) % ny) * nz + (z + o[1]) % nz, ((x + o[2]) % (nx // 2)) * 2 + (core + o[3]) % 2)
            for o in kept
        ]

    one_hop = peers(
        [(0, 1, 0, 0), (0, -1, 0, 0), (1, 0, 0, 0), (-1, 0, 0, 0), (0, 0, 1, 0), (0, 0, -1, 0), (0, 0, 0, 1)]
    )
    two_hops = peers([(0, 2, 0, 0), (0, -2, 0, 0), (2, 0, 0, 0), (0, 0, 2, 0)])
    four_hops = peers([(0, 4, 0, 0), (0, -4, 0, 0), (0, 0, 0, 1)])
    plane = [(j, 0, i, c) for j in range(ny) for i in range(nx // 2) for c in range(2)]
    line = [(0, i, 0, 0) for i in range(nz)]
    far_first = lambda o: -sum(min(d, n - d) for d, n in zip(o, (ny, nz, nx // 2, 2)))
    groups = [peers(sorted(plane, key=far_first)), peers(sorted(line, key=far_first))]

    barrier = pltpu.get_barrier_semaphore()
    met = [after, before, below, above] + one_hop
    for peer in met:
        pl.semaphore_signal(barrier, inc=1, device_id=peer, device_id_type=MESH)

    def greet(stage, who):
        for peer in who:
            pl.semaphore_signal(greet_sem.at[stage], inc=1, device_id=peer, device_id_type=MESH)

    loads = [
        pltpu.make_async_copy(src, dst, load_sem.at[i])
        for i, (src, dst) in enumerate(
            [
                (count_hbm, count_ref),
                (weight_hbm, weight_ref),
                (source_hbm, source_ref),
                (rhs_hbm, rhs_ref),
                (down_hbm, down_ref),
                (across_hbm, across_ref),
                (anchor_hbm, anchor_ref),
                (target_hbm, target_ref),
            ]
        )
    ]
    for load in loads:
        load.start()

    sent, kept = [], []

    def send(src, dst, peer, index):
        copy = pltpu.make_async_remote_copy(
            src_ref=src,
            dst_ref=dst,
            send_sem=send_sem.at[index],
            recv_sem=recv_sem.at[index],
            device_id=peer,
            device_id_type=MESH,
        )
        copy.start()
        sent.append(copy)
        return copy

    slot = lax.broadcasted_iota(jnp.int32, (1, slots), 1)
    loads[0].wait()
    loads[1].wait()
    live = ((slot < count_ref[0, 0] * BLOCK) & (gz < n_gz - 1)).astype(jnp.float32)
    for k in range(4):
        slot_out[k] = weight_ref[k, 0] * live
    loads[7].wait()
    slot_out[4] = target_ref[0].astype(jnp.float32)
    def post_halo(field, k):
        for c in range(2):
            halo_out[k, 0, c : c + 1, :] = field[c][:1]
            halo_out[k, 1, c : c + 1, :] = field[c][rows - 1 :]
        return [
            send(halo_out.at[k, 0], halo_in.at[k, 0], above, 2 + 4 * k),
            send(halo_out.at[k, 1], halo_in.at[k, 1], below, 3 + 4 * k),
        ]

    pl.semaphore_wait(barrier, len(met))
    copies = [
        send(slot_out, slot_in, after, 0),
    ]
    greet(0, one_hop)

    loads[3].wait()
    field = [rhs_ref[c, 0] for c in range(2)]
    halo = post_halo(field, 0)
    loads[4].wait()
    rim_out[...] = down_ref[0, rows - 1 :]
    copies.append(send(rim_out, rim_in, below, 1))

    low_id = lax.broadcasted_iota(jnp.int32, (LOW, slots), 0)
    place_id = lax.broadcasted_iota(jnp.int32, (highs * rows, slots), 0)

    def split(node):
        col = node & (cols - 1)
        return col & (LOW - 1), (col >> bits_low) * rows + (node >> bits_cols)

    loads[2].wait()
    low, place = split(source_ref[0])
    hot_source[...] = (low_id == low).astype(jnp.float32).astype(jnp.bfloat16)
    mask_source[...] = jnp.where(place_id == place, live, 0.0)


    loads[5].wait()
    loads[6].wait()
    across, down, anchor = across_ref[0], down_ref[0], anchor_ref[0]
    col_id = lax.broadcasted_iota(jnp.int32, (rows, cols), 1)
    row_id = lax.broadcasted_iota(jnp.int32, (rows, cols), 0)
    products = []

    for k in range(ITERS):
        base = 2 + 4 * k
        own = looked_up(pieces(stacked(field), 3), hot_source, [mask_source], 3)
        for c in range(2):
            point_out[k, 0, c : c + 1, :] = own[c]
        own_copy = send(point_out.at[k, 0], point_in.at[k, 0], after, base + 2)
        right = [jnp.where(col_id == cols - 1, 0.0, pltpu.roll(f, cols - 1, 1)) for f in field]
        if k == 0:
            copies[0].wait_recv()
            low, place = split(slot_in[4].astype(jnp.int32))
            hot_target[...] = (low_id == low).astype(jnp.float32).astype(jnp.bfloat16)
            for mask, one, two in ((mask_left, 0, 2), (mask_right, 1, 3)):
                mask[...] = jnp.where(
                    place_id == place,
                    slot_in[one],
                    jnp.where(place_id == place + 1, slot_in[two], 0.0),
                )
        table = jnp.concatenate([pieces(stacked(field), 3), pieces(stacked(right), 3)], 0)
        there = looked_up(table, hot_target, [mask_left, mask_right], 3)
        for c in range(2):
            point_out[k, 1, c : c + 1, :] = there[c]
        there_copy = send(point_out.at[k, 1], point_in.at[k, 1], before, base + 3)

        image, energy = [], None
        for c in range(2):
            f = field[c]
            gap = f - right[c]
            flux = across * gap
            fall = jnp.where(row_id == rows - 1, 0.0, f - pltpu.roll(f, rows - 1, 0))
            drop = down * fall
            held = anchor * f
            come = jnp.where(col_id == 0, 0.0, pltpu.roll(flux, 1, 1))
            above_me = jnp.where(row_id == 0, 0.0, pltpu.roll(drop, 1, 0))
            image.append(flux - come + drop - above_me + held)
            if k == ITERS - 1:
                term = flux * gap + drop * fall + held * f
                energy = term if energy is None else energy + term
        if k > 0:
            products.append(sum(folded(a * b) for a, b in zip(former, field)))
        products.append(sum(folded(a * a) for a in field))
        if k == ITERS - 1:
            rows_known = [jnp.sum(p, 0, keepdims=True) for p in products]
            energy = folded(energy)

        if k == 0:
            pl.semaphore_wait(greet_sem.at[0], len(one_hop))
            greet(1, two_hops)
        if k == 1:
            pl.semaphore_wait(greet_sem.at[1], len(two_hops))
            greet(2, four_hops)

        def onward():
            own_copy.wait_recv()
            error_in = [there[c] - point_in[k, 0, c : c + 1, :] for c in range(2)]
            left = unstacked(spread(error_in, mask_left, hot_target, 2), rows, highs)
            more = unstacked(spread(error_in, mask_right, hot_target, 2), rows, highs)
            return [a + pltpu.roll(b, 1, 1) for a, b in zip(left, more)]

        if k < ITERS - 1:
            image = [a + b for a, b in zip(image, onward())]

        if k == 0:
            copies[1].wait_recv()
        halo[0].wait_recv()
        halo[1].wait_recv()
        rim = jnp.where(xy > 0, rim_in[...], 0.0)
        for c in range(2):
            f = field[c]
            upper = halo_in[k, 1, c : c + 1, :]
            lower = jnp.where(xy < nx - 1, halo_in[k, 0, c : c + 1, :], 0.0)
            fall = f - lower
            drop = down * fall
            edge = jnp.where(row_id == 0, rim * (f - upper), 0.0)
            image[c] = image[c] + jnp.where(row_id == rows - 1, drop + edge, edge)
            if k == ITERS - 1:
                energy = energy + folded(jnp.where(row_id == rows - 1, drop * fall, 0.0))

        there_copy.wait_recv()
        error = [point_in[k, 1, c : c + 1, :] - own[c] for c in range(2)]
        if k == ITERS - 1:
            tie = sum(e * e for e in error)
            last = jnp.sum(energy, 0, keepdims=True) + folded(tie)
            rows_known.append(last * (1.0 / SCALE))
            rows_known.append(jnp.zeros((8 - MOMENTS, 128), jnp.float32))
            lanes = jnp.concatenate(rows_known, 0)
            eight = lax.broadcasted_iota(jnp.int32, (8, 128), 0)
            total = jnp.sum(lanes, 1, keepdims=True)
            lane = lax.broadcasted_iota(jnp.int32, (8, 128), 1)
            total = jnp.sum(jnp.where(lane == eight, total, 0.0), 0, keepdims=True)

        def post_sum(stage, total):
            sums[stage, 0] = total
            if stage == 0:
                pl.semaphore_wait(greet_sem.at[2], len(four_hops))
            index = 2 + 4 * ITERS + stage
            for i, peer in enumerate(groups[stage]):
                copy = pltpu.make_async_remote_copy(
                    src_ref=sums.at[stage, 0],
                    dst_ref=sums.at[stage, i + 1],
                    send_sem=send_sem.at[index],
                    recv_sem=recv_sem.at[index],
                    device_id=peer,
                    device_id_type=MESH,
                )
                copy.start()

        def take_sum(stage):
            index = 2 + 4 * ITERS + stage
            count = len(groups[stage])
            arrived = sums.at[stage, pl.ds(1, count)]
            pltpu.make_async_copy(arrived, arrived, recv_sem.at[index]).wait()
            return functools.reduce(lambda a, b: a + b, [sums[stage, i] for i in range(count + 1)])

        if k == ITERS - 1:
            post_sum(0, total)
            image = [a + b for a, b in zip(image, onward())]
        back = unstacked(spread(error, mask_source, hot_source, 2), rows, highs)
        latest = [(a - b) * (1.0 / SCALE) for a, b in zip(image, back)]
        if k < ITERS - 1:
            halo = post_halo(latest, k + 1)
        for c in range(2):
            basis[k, c] = latest[c]
        keep = pltpu.make_async_copy(basis.at[k], basis_hbm.at[k], keep_sem.at[k])
        keep.start()
        kept.append(keep)
        former, field = field, latest

    post_sum(1, take_sum(0))
    total = take_sum(1)
    lane = lax.broadcasted_iota(jnp.int32, (1, 128), 1)
    mu = [
        jnp.sum(jnp.where(lane == i, total, 0.0), 1, keepdims=True) for i in range(MOMENTS)
    ]
    steps, rest = coefficients(mu)
    rows_of = [jnp.broadcast_to(s, (1, 128)) for s in [s * (1.0 / SCALE) for s in steps] + rest[1:]]
    scalars[...] = jnp.concatenate(rows_of + [jnp.zeros((8 - 2 * ITERS, 128), jnp.float32)], 0)

    for keep in kept:
        keep.wait()
    for copy in sent:
        copy.wait_send()
    for stage in range(2):
        count = len(groups[stage])
        gone = sums.at[stage, pl.ds(1, count)]
        pltpu.make_async_copy(gone, gone, send_sem.at[2 + 4 * ITERS + stage]).wait()


def combine(rhs_hbm, basis_hbm, scalars_hbm, x_hbm, r_hbm, rhs, basis, scalars, x, r, load_sem, save_sem):
    loads = [
        pltpu.make_async_copy(src, dst, load_sem.at[i])
        for i, (src, dst) in enumerate(((scalars_hbm, scalars), (rhs_hbm, rhs), (basis_hbm, basis)))
    ]
    for load in loads:
        load.start()
    for load in loads:
        load.wait()
    values = [scalars[i : i + 1, :1] for i in range(2 * ITERS)]
    saves = []
    for c in range(2):
        powers = [rhs[c, 0]] + [basis[i, c] for i in range(ITERS)]
        x[c, 0] = sum(s * v for s, v in zip(values[:ITERS], powers))
        r[c, 0] = powers[0] + sum(s * v for s, v in zip(values[ITERS:], powers[1:]))
        for n, (src, dst) in enumerate(((x, x_hbm), (r, r_hbm))):
            save = pltpu.make_async_copy(src.at[c], dst.at[c], save_sem.at[2 * c + n])
            save.start()
            saves.append(save)
    for save in saves:
        save.wait()


def body(nz, rhs, across, down, anchor, source, target, weight, count):
    n_gz, nx = lax.axis_size("gz"), lax.axis_size("xy")
    ny = n_gz // nz
    rows, cols = across.shape[1:]
    slots = source.shape[2]
    places = rows * cols // LOW
    f32, bf16 = jnp.float32, jnp.bfloat16
    vmem = pl.BlockSpec(memory_space=pltpu.VMEM)
    hbm = pl.BlockSpec(memory_space=pltpu.HBM)
    args = (rhs, across, down, anchor, source, target, weight, count)
    copies = 2 + 4 * ITERS + 2
    widest = max(nx * ny, nz)
    basis, scalars = pl.pallas_call(
        functools.partial(kernel, ny, nz, nx),
        out_shape=(
            jax.ShapeDtypeStruct((ITERS, 2, rows, cols), f32),
            jax.ShapeDtypeStruct((8, 128), f32),
        ),
        in_specs=[hbm] * len(args),
        out_specs=(hbm, vmem),
        scratch_shapes=[
            pltpu.VMEM(rhs.shape, f32),
            pltpu.VMEM(across.shape, f32),
            pltpu.VMEM(down.shape, f32),
            pltpu.VMEM(anchor.shape, f32),
            pltpu.VMEM(source.shape, jnp.int32),
            pltpu.VMEM(target.shape, jnp.int32),
            pltpu.VMEM(weight.shape, f32),
            pltpu.SMEM(count.shape, jnp.int32),
            pltpu.VMEM((LOW, slots), bf16),
            pltpu.VMEM((LOW, slots), bf16),
            pltpu.VMEM((places, slots), f32),
            pltpu.VMEM((places, slots), f32),
            pltpu.VMEM((places, slots), f32),
            pltpu.VMEM((ITERS, 2, rows, cols), f32),
            pltpu.VMEM((5, 1, slots), f32),
            pltpu.VMEM((1, cols), f32),
            pltpu.VMEM((ITERS, 2, 2, cols), f32),
            pltpu.VMEM((ITERS, 2, 2, slots), f32),
            pltpu.VMEM((5, 1, slots), f32),
            pltpu.VMEM((1, cols), f32),
            pltpu.VMEM((ITERS, 2, 2, cols), f32),
            pltpu.VMEM((ITERS, 2, 2, slots), f32),
            pltpu.VMEM((2, widest, 1, 128), f32),
            pltpu.SemaphoreType.DMA((copies,)),
            pltpu.SemaphoreType.DMA((copies,)),
            pltpu.SemaphoreType.DMA((8,)),
            pltpu.SemaphoreType.DMA((ITERS,)),
            pltpu.SemaphoreType.REGULAR((3,)),
        ],
        compiler_params=pltpu.CompilerParams(
            collective_id=0, has_side_effects=True, vmem_limit_bytes=63 * 1024 * 1024
        ),
    )(*args)
    out = jax.ShapeDtypeStruct(rhs.shape, f32)
    return pl.pallas_call(
        combine,
        out_shape=(out, out),
        in_specs=[hbm] * 3,
        out_specs=(hbm, hbm),
        scratch_shapes=[
            pltpu.VMEM(rhs.shape, f32),
            pltpu.VMEM(basis.shape, f32),
            pltpu.VMEM(scalars.shape, f32),
            pltpu.VMEM(rhs.shape, f32),
            pltpu.VMEM(rhs.shape, f32),
            pltpu.SemaphoreType.DMA((3,)),
            pltpu.SemaphoreType.DMA((4,)),
        ],
        compiler_params=pltpu.CompilerParams(vmem_limit_bytes=63 * 1024 * 1024),
    )(rhs, basis, scalars)


def solution(mesh, nz=16):
    in_specs = (
        P(None, "gz", "xy", None),
        P("gz", "xy", None),
        P("gz", "xy", None),
        P("gz", "xy", None),
        P("gz", "xy", None),
        P("gz", "xy", None),
        P(None, "gz", "xy", None),
        P("gz", "xy"),
    )
    out_specs = (P(None, "gz", "xy", None), P(None, "gz", "xy", None))
    return jax.shard_map(
        functools.partial(body, nz), mesh=mesh, in_specs=in_specs, out_specs=out_specs, check_vma=False
    )
```

```python
import functools

import jax
import jax.numpy as jnp
from jax import lax
from jax.experimental import pallas as pl
from jax.experimental.pallas import tpu as pltpu
from jax.sharding import PartitionSpec as P

BLOCK = 128
ITERS = 3
LOW = 256
SCALE = 8.0
MESH = pl.DeviceIdType.MESH
MOMENTS = 2 * ITERS


def pieces(values, count):
    out = []
    for i in range(count):
        part = values.astype(jnp.bfloat16)
        out.append(part)
        if i + 1 < count:
            values = values - part.astype(jnp.float32)
    return jnp.concatenate(out, 0)


def summed(pieces_of, count):
    rows = pieces_of.shape[0] // count
    total = pieces_of[:rows]
    for i in range(1, count):
        total = total + pieces_of[i * rows : (i + 1) * rows]
    return total


def stacked(field):
    return jnp.concatenate(
        [part[:, h : h + LOW] for part in field for h in range(0, part.shape[1], LOW)], 0
    )


def unstacked(table, rows, highs):
    return [
        jnp.concatenate(
            [table[(c * highs + h) * rows : (c * highs + h + 1) * rows] for h in range(highs)], 1
        )
        for c in range(2)
    ]


def looked_up(table, hot, masks, first):
    wide = hot.shape[1]
    cut = min(wide, 256)
    out = []
    for j in range(0, wide, cut):
        found = jnp.dot(table, hot[:, j : j + cut], preferred_element_type=jnp.float32)
        out.append([])
        per = found.shape[0] // len(masks)
        totals = None
        for m, mask in enumerate(masks):
            got = summed(found[m * per : (m + 1) * per], first)
            half = got.shape[0] // 2
            terms = [got[c * half : (c + 1) * half] * mask[:, j : j + cut] for c in range(2)]
            totals = terms if totals is None else [a + b for a, b in zip(totals, terms)]
        out[-1] = [jnp.sum(t, 0, keepdims=True) for t in totals]
    return [jnp.concatenate([o[c] for o in out], 1) for c in range(2)]


def spread(errors, mask, hot, count):
    table = jnp.concatenate([mask[...] * e for e in errors], 0)
    out = lax.dot_general(
        pieces(table, count), hot[...], (((1,), (1,)), ((), ())), preferred_element_type=jnp.float32
    )
    return summed(out, count)


def folded(values):
    return sum(values[:, i : i + 128] for i in range(0, values.shape[1], 128))


def coefficients(mu):
    def inner(a, b, shift):
        total = None
        for i, x in enumerate(a):
            for j, y in enumerate(b):
                term = mu[i + j + shift]
                if x is not None:
                    term = x * term
                if y is not None:
                    term = y * term
                total = term if total is None else total + term
        return total

    residual, direction, field = [None], [None], []
    norm = mu[0]
    for step in range(ITERS):
        alpha = norm / inner(direction, direction, 1)
        along = [alpha if d is None else alpha * d for d in direction]
        field = [a if i >= len(field) else field[i] + a for i, a in enumerate(along)]
        residual = residual[:1] + [
            -a if i + 1 >= len(residual) else residual[i + 1] - a for i, a in enumerate(along)
        ]
        if step + 1 < ITERS:
            fresh = inner(residual, residual, 0)
            ratio = fresh / norm
            step_of = [ratio if d is None else ratio * d for d in direction]
            direction = [
                (1.0 if r is None else r) + (step_of[i] if i < len(step_of) else 0.0)
                for i, r in enumerate(residual)
            ]
            norm = fresh
    return field, residual


def kernel(
    ny,
    nz,
    nx,
    rhs_hbm,
    across_hbm,
    down_hbm,
    anchor_hbm,
    source_hbm,
    target_hbm,
    weight_hbm,
    count_hbm,
    basis_hbm,
    scalars,
    rhs_ref,
    across_ref,
    down_ref,
    anchor_ref,
    source_ref,
    target_ref,
    weight_ref,
    count_ref,
    hot_source,
    hot_target,
    mask_source,
    mask_left,
    mask_right,
    basis,
    slot_out,
    rim_out,
    halo_out,
    point_out,
    slot_in,
    rim_in,
    halo_in,
    point_in,
    sums,
    send_sem,
    recv_sem,
    load_sem,
    keep_sem,
    greet_sem,
):
    rows, cols = across_ref.shape[1:]
    slots = source_ref.shape[2]
    highs = cols // LOW
    bits_cols, bits_low = cols.bit_length() - 1, LOW.bit_length() - 1
    n_gz = ny * nz
    gz, xy = lax.axis_index("gz"), lax.axis_index("xy")
    y, z, x, core = gz // nz, gz % nz, xy // 2, xy % 2
    after, before = ((gz + 1) % n_gz, xy), ((gz + n_gz - 1) % n_gz, xy)
    below, above = (gz, (xy + 1) % nx), (gz, (xy + nx - 1) % nx)

    def peers(offsets):
        sizes = (ny, nz, nx // 2, 2)
        kept = []
        for offset in offsets:
            offset = tuple(o % n for o, n in zip(offset, sizes))
            if any(offset) and offset not in kept:
                kept.append(offset)
        return [
            (((y + o[0]) % ny) * nz + (z + o[1]) % nz, ((x + o[2]) % (nx // 2)) * 2 + (core + o[3]) % 2)
            for o in kept
        ]

    one_hop = peers(
        [(0, 1, 0, 0), (0, -1, 0, 0), (1, 0, 0, 0), (-1, 0, 0, 0), (0, 0, 1, 0), (0, 0, -1, 0), (0, 0, 0, 1)]
    )
    two_hops = peers([(0, 2, 0, 0), (0, -2, 0, 0), (2, 0, 0, 0), (0, 0, 2, 0)])
    four_hops = peers([(0, 4, 0, 0), (0, -4, 0, 0), (0, 0, 0, 1)])
    plane = [(j, 0, i, c) for j in range(ny) for i in range(nx // 2) for c in range(2)]
    line = [(0, i, 0, 0) for i in range(nz)]
    far_first = lambda o: -sum(min(d, n - d) for d, n in zip(o, (ny, nz, nx // 2, 2)))
    groups = [peers(sorted(plane, key=far_first)), peers(sorted(line, key=far_first))]

    barrier = pltpu.get_barrier_semaphore()
    met = [after, before, below, above] + one_hop
    for peer in met:
        pl.semaphore_signal(barrier, inc=1, device_id=peer, device_id_type=MESH)

    def greet(stage, who):
        for peer in who:
            pl.semaphore_signal(greet_sem.at[stage], inc=1, device_id=peer, device_id_type=MESH)

    loads = [
        pltpu.make_async_copy(src, dst, load_sem.at[i])
        for i, (src, dst) in enumerate(
            [
                (count_hbm, count_ref),
                (weight_hbm, weight_ref),
                (source_hbm, source_ref),
                (rhs_hbm, rhs_ref),
                (down_hbm, down_ref),
                (across_hbm, across_ref),
                (anchor_hbm, anchor_ref),
                (target_hbm, target_ref),
            ]
        )
    ]
    for load in loads:
        load.start()

    sent, kept = [], []

    def send(src, dst, peer, index):
        copy = pltpu.make_async_remote_copy(
            src_ref=src,
            dst_ref=dst,
            send_sem=send_sem.at[index],
            recv_sem=recv_sem.at[index],
            device_id=peer,
            device_id_type=MESH,
        )
        copy.start()
        sent.append(copy)
        return copy

    slot = lax.broadcasted_iota(jnp.int32, (1, slots), 1)
    loads[0].wait()
    loads[1].wait()
    live = ((slot < count_ref[0, 0] * BLOCK) & (gz < n_gz - 1)).astype(jnp.float32)
    for k in range(4):
        slot_out[k] = weight_ref[k, 0] * live
    loads[7].wait()
    slot_out[4] = target_ref[0].astype(jnp.float32)
    def post_halo(field, k):
        for c in range(2):
            halo_out[k, 0, c : c + 1, :] = field[c][:1]
            halo_out[k, 1, c : c + 1, :] = field[c][rows - 1 :]
        return [
            send(halo_out.at[k, 0], halo_in.at[k, 0], above, 2 + 4 * k),
            send(halo_out.at[k, 1], halo_in.at[k, 1], below, 3 + 4 * k),
        ]

    pl.semaphore_wait(barrier, len(met))
    copies = [
        send(slot_out, slot_in, after, 0),
    ]
    greet(0, one_hop)

    loads[3].wait()
    field = [rhs_ref[c, 0] for c in range(2)]
    halo = post_halo(field, 0)
    loads[4].wait()
    rim_out[...] = down_ref[0, rows - 1 :]
    copies.append(send(rim_out, rim_in, below, 1))

    low_id = lax.broadcasted_iota(jnp.int32, (LOW, slots), 0)
    place_id = lax.broadcasted_iota(jnp.int32, (highs * rows, slots), 0)

    def split(node):
        col = node & (cols - 1)
        return col & (LOW - 1), (col >> bits_low) * rows + (node >> bits_cols)

    loads[2].wait()
    low, place = split(source_ref[0])
    hot_source[...] = (low_id == low).astype(jnp.float32).astype(jnp.bfloat16)
    mask_source[...] = jnp.where(place_id == place, live, 0.0)


    loads[5].wait()
    loads[6].wait()
    across, down, anchor = across_ref[0], down_ref[0], anchor_ref[0]
    col_id = lax.broadcasted_iota(jnp.int32, (rows, cols), 1)
    row_id = lax.broadcasted_iota(jnp.int32, (rows, cols), 0)
    products = []

    for k in range(ITERS):
        base = 2 + 4 * k
        own = looked_up(pieces(stacked(field), 2), hot_source, [mask_source], 2)
        for c in range(2):
            point_out[k, 0, c : c + 1, :] = own[c]
        own_copy = send(point_out.at[k, 0], point_in.at[k, 0], after, base + 2)
        right = [jnp.where(col_id == cols - 1, 0.0, pltpu.roll(f, cols - 1, 1)) for f in field]
        if k == 0:
            copies[0].wait_recv()
            low, place = split(slot_in[4].astype(jnp.int32))
            hot_target[...] = (low_id == low).astype(jnp.float32).astype(jnp.bfloat16)
            for mask, one, two in ((mask_left, 0, 2), (mask_right, 1, 3)):
                mask[...] = jnp.where(
                    place_id == place,
                    slot_in[one],
                    jnp.where(place_id == place + 1, slot_in[two], 0.0),
                )
        table = jnp.concatenate([pieces(stacked(field), 2), pieces(stacked(right), 2)], 0)
        there = looked_up(table, hot_target, [mask_left, mask_right], 2)
        for c in range(2):
            point_out[k, 1, c : c + 1, :] = there[c]
        there_copy = send(point_out.at[k, 1], point_in.at[k, 1], before, base + 3)

        image, energy = [], None
        for c in range(2):
            f = field[c]
            gap = f - right[c]
            flux = across * gap
            fall = jnp.where(row_id == rows - 1, 0.0, f - pltpu.roll(f, rows - 1, 0))
            drop = down * fall
            held = anchor * f
            come = jnp.where(col_id == 0, 0.0, pltpu.roll(flux, 1, 1))
            above_me = jnp.where(row_id == 0, 0.0, pltpu.roll(drop, 1, 0))
            image.append(flux - come + drop - above_me + held)
            if k == ITERS - 1:
                term = flux * gap + drop * fall + held * f
                energy = term if energy is None else energy + term
        if k > 0:
            products.append(sum(folded(a * b) for a, b in zip(former, field)))
        products.append(sum(folded(a * a) for a in field))
        if k == ITERS - 1:
            rows_known = [jnp.sum(p, 0, keepdims=True) for p in products]
            energy = folded(energy)

        if k == 0:
            pl.semaphore_wait(greet_sem.at[0], len(one_hop))
            greet(1, two_hops)
        if k == 1:
            pl.semaphore_wait(greet_sem.at[1], len(two_hops))
            greet(2, four_hops)

        def onward():
            own_copy.wait_recv()
            error_in = [there[c] - point_in[k, 0, c : c + 1, :] for c in range(2)]
            left = unstacked(spread(error_in, mask_left, hot_target, 2), rows, highs)
            more = unstacked(spread(error_in, mask_right, hot_target, 2), rows, highs)
            return [a + pltpu.roll(b, 1, 1) for a, b in zip(left, more)]

        if k < ITERS - 1:
            image = [a + b for a, b in zip(image, onward())]

        if k == 0:
            copies[1].wait_recv()
        halo[0].wait_recv()
        halo[1].wait_recv()
        rim = jnp.where(xy > 0, rim_in[...], 0.0)
        for c in range(2):
            f = field[c]
            upper = halo_in[k, 1, c : c + 1, :]
            lower = jnp.where(xy < nx - 1, halo_in[k, 0, c : c + 1, :], 0.0)
            fall = f - lower
            drop = down * fall
            edge = jnp.where(row_id == 0, rim * (f - upper), 0.0)
            image[c] = image[c] + jnp.where(row_id == rows - 1, drop + edge, edge)
            if k == ITERS - 1:
                energy = energy + folded(jnp.where(row_id == rows - 1, drop * fall, 0.0))

        there_copy.wait_recv()
        error = [point_in[k, 1, c : c + 1, :] - own[c] for c in range(2)]
        if k == ITERS - 1:
            tie = sum(e * e for e in error)
            last = jnp.sum(energy, 0, keepdims=True) + folded(tie)
            rows_known.append(last * (1.0 / SCALE))
            rows_known.append(jnp.zeros((8 - MOMENTS, 128), jnp.float32))
            lanes = jnp.concatenate(rows_known, 0)
            eight = lax.broadcasted_iota(jnp.int32, (8, 128), 0)
            total = jnp.sum(lanes, 1, keepdims=True)
            lane = lax.broadcasted_iota(jnp.int32, (8, 128), 1)
            total = jnp.sum(jnp.where(lane == eight, total, 0.0), 0, keepdims=True)

        def post_sum(stage, total):
            sums[stage, 0] = total
            if stage == 0:
                pl.semaphore_wait(greet_sem.at[2], len(four_hops))
            index = 2 + 4 * ITERS + stage
            for i, peer in enumerate(groups[stage]):
                copy = pltpu.make_async_remote_copy(
                    src_ref=sums.at[stage, 0],
                    dst_ref=sums.at[stage, i + 1],
                    send_sem=send_sem.at[index],
                    recv_sem=recv_sem.at[index],
                    device_id=peer,
                    device_id_type=MESH,
                )
                copy.start()

        def take_sum(stage):
            index = 2 + 4 * ITERS + stage
            count = len(groups[stage])
            arrived = sums.at[stage, pl.ds(1, count)]
            pltpu.make_async_copy(arrived, arrived, recv_sem.at[index]).wait()
            return functools.reduce(lambda a, b: a + b, [sums[stage, i] for i in range(count + 1)])

        if k == ITERS - 1:
            post_sum(0, total)
            image = [a + b for a, b in zip(image, onward())]
        back = unstacked(spread(error, mask_source, hot_source, 2), rows, highs)
        latest = [(a - b) * (1.0 / SCALE) for a, b in zip(image, back)]
        if k < ITERS - 1:
            halo = post_halo(latest, k + 1)
        for c in range(2):
            basis[k, c] = latest[c]
        keep = pltpu.make_async_copy(basis.at[k], basis_hbm.at[k], keep_sem.at[k])
        keep.start()
        kept.append(keep)
        former, field = field, latest

    post_sum(1, take_sum(0))
    total = take_sum(1)
    lane = lax.broadcasted_iota(jnp.int32, (1, 128), 1)
    mu = [
        jnp.sum(jnp.where(lane == i, total, 0.0), 1, keepdims=True) for i in range(MOMENTS)
    ]
    steps, rest = coefficients(mu)
    rows_of = [jnp.broadcast_to(s, (1, 128)) for s in [s * (1.0 / SCALE) for s in steps] + rest[1:]]
    scalars[...] = jnp.concatenate(rows_of + [jnp.zeros((8 - 2 * ITERS, 128), jnp.float32)], 0)

    for keep in kept:
        keep.wait()
    for copy in sent:
        copy.wait_send()
    for stage in range(2):
        count = len(groups[stage])
        gone = sums.at[stage, pl.ds(1, count)]
        pltpu.make_async_copy(gone, gone, send_sem.at[2 + 4 * ITERS + stage]).wait()


def combine(rhs_hbm, basis_hbm, scalars_hbm, x_hbm, r_hbm, rhs, basis, scalars, x, r, load_sem, save_sem):
    loads = [
        pltpu.make_async_copy(src, dst, load_sem.at[i])
        for i, (src, dst) in enumerate(((scalars_hbm, scalars), (rhs_hbm, rhs), (basis_hbm, basis)))
    ]
    for load in loads:
        load.start()
    for load in loads:
        load.wait()
    values = [scalars[i : i + 1, :1] for i in range(2 * ITERS)]
    saves = []
    for c in range(2):
        powers = [rhs[c, 0]] + [basis[i, c] for i in range(ITERS)]
        x[c, 0] = sum(s * v for s, v in zip(values[:ITERS], powers))
        r[c, 0] = powers[0] + sum(s * v for s, v in zip(values[ITERS:], powers[1:]))
        for n, (src, dst) in enumerate(((x, x_hbm), (r, r_hbm))):
            save = pltpu.make_async_copy(src.at[c], dst.at[c], save_sem.at[2 * c + n])
            save.start()
            saves.append(save)
    for save in saves:
        save.wait()


def body(nz, rhs, across, down, anchor, source, target, weight, count):
    n_gz, nx = lax.axis_size("gz"), lax.axis_size("xy")
    ny = n_gz // nz
    rows, cols = across.shape[1:]
    slots = source.shape[2]
    places = rows * cols // LOW
    f32, bf16 = jnp.float32, jnp.bfloat16
    vmem = pl.BlockSpec(memory_space=pltpu.VMEM)
    hbm = pl.BlockSpec(memory_space=pltpu.HBM)
    args = (rhs, across, down, anchor, source, target, weight, count)
    copies = 2 + 4 * ITERS + 2
    widest = max(nx * ny, nz)
    basis, scalars = pl.pallas_call(
        functools.partial(kernel, ny, nz, nx),
        out_shape=(
            jax.ShapeDtypeStruct((ITERS, 2, rows, cols), f32),
            jax.ShapeDtypeStruct((8, 128), f32),
        ),
        in_specs=[hbm] * len(args),
        out_specs=(hbm, vmem),
        scratch_shapes=[
            pltpu.VMEM(rhs.shape, f32),
            pltpu.VMEM(across.shape, f32),
            pltpu.VMEM(down.shape, f32),
            pltpu.VMEM(anchor.shape, f32),
            pltpu.VMEM(source.shape, jnp.int32),
            pltpu.VMEM(target.shape, jnp.int32),
            pltpu.VMEM(weight.shape, f32),
            pltpu.SMEM(count.shape, jnp.int32),
            pltpu.VMEM((LOW, slots), bf16),
            pltpu.VMEM((LOW, slots), bf16),
            pltpu.VMEM((places, slots), f32),
            pltpu.VMEM((places, slots), f32),
            pltpu.VMEM((places, slots), f32),
            pltpu.VMEM((ITERS, 2, rows, cols), f32),
            pltpu.VMEM((5, 1, slots), f32),
            pltpu.VMEM((1, cols), f32),
            pltpu.VMEM((ITERS, 2, 2, cols), f32),
            pltpu.VMEM((ITERS, 2, 2, slots), f32),
            pltpu.VMEM((5, 1, slots), f32),
            pltpu.VMEM((1, cols), f32),
            pltpu.VMEM((ITERS, 2, 2, cols), f32),
            pltpu.VMEM((ITERS, 2, 2, slots), f32),
            pltpu.VMEM((2, widest, 1, 128), f32),
            pltpu.SemaphoreType.DMA((copies,)),
            pltpu.SemaphoreType.DMA((copies,)),
            pltpu.SemaphoreType.DMA((8,)),
            pltpu.SemaphoreType.DMA((ITERS,)),
            pltpu.SemaphoreType.REGULAR((3,)),
        ],
        compiler_params=pltpu.CompilerParams(
            collective_id=0, has_side_effects=True, vmem_limit_bytes=63 * 1024 * 1024
        ),
    )(*args)
    out = jax.ShapeDtypeStruct(rhs.shape, f32)
    return pl.pallas_call(
        combine,
        out_shape=(out, out),
        in_specs=[hbm] * 3,
        out_specs=(hbm, hbm),
        scratch_shapes=[
            pltpu.VMEM(rhs.shape, f32),
            pltpu.VMEM(basis.shape, f32),
            pltpu.VMEM(scalars.shape, f32),
            pltpu.VMEM(rhs.shape, f32),
            pltpu.VMEM(rhs.shape, f32),
            pltpu.SemaphoreType.DMA((3,)),
            pltpu.SemaphoreType.DMA((4,)),
        ],
        compiler_params=pltpu.CompilerParams(vmem_limit_bytes=63 * 1024 * 1024),
    )(rhs, basis, scalars)


def solution(mesh, nz=16):
    in_specs = (
        P(None, "gz", "xy", None),
        P("gz", "xy", None),
        P("gz", "xy", None),
        P("gz", "xy", None),
        P("gz", "xy", None),
        P("gz", "xy", None),
        P(None, "gz", "xy", None),
        P("gz", "xy"),
    )
    out_specs = (P(None, "gz", "xy", None), P(None, "gz", "xy", None))
    return jax.shard_map(
        functools.partial(body, nz), mesh=mesh, in_specs=in_specs, out_specs=out_specs, check_vma=False
    )
```

```python
import functools

import jax
import jax.numpy as jnp
from jax import lax
from jax.experimental import pallas as pl
from jax.experimental.pallas import tpu as pltpu
from jax.sharding import PartitionSpec as P

BLOCK = 128
ITERS = 3
LOW = 256
SCALE = 8.0
MESH = pl.DeviceIdType.MESH
MOMENTS = 2 * ITERS


def pieces(values, count):
    out = []
    for i in range(count):
        part = values.astype(jnp.bfloat16)
        out.append(part)
        if i + 1 < count:
            values = values - part.astype(jnp.float32)
    return jnp.concatenate(out, 0)


def summed(pieces_of, count):
    rows = pieces_of.shape[0] // count
    total = pieces_of[:rows]
    for i in range(1, count):
        total = total + pieces_of[i * rows : (i + 1) * rows]
    return total


def stacked(field):
    return jnp.concatenate(
        [part[:, h : h + LOW] for part in field for h in range(0, part.shape[1], LOW)], 0
    )


def unstacked(table, rows, highs):
    return [
        jnp.concatenate(
            [table[(c * highs + h) * rows : (c * highs + h + 1) * rows] for h in range(highs)], 1
        )
        for c in range(2)
    ]


def looked_up(table, hot, masks, first):
    wide = hot.shape[1]
    cut = min(wide, 256)
    out = []
    for j in range(0, wide, cut):
        found = jnp.dot(table, hot[:, j : j + cut], preferred_element_type=jnp.float32)
        out.append([])
        per = found.shape[0] // len(masks)
        totals = None
        for m, mask in enumerate(masks):
            got = summed(found[m * per : (m + 1) * per], first)
            half = got.shape[0] // 2
            terms = [got[c * half : (c + 1) * half] * mask[:, j : j + cut] for c in range(2)]
            totals = terms if totals is None else [a + b for a, b in zip(totals, terms)]
        out[-1] = [jnp.sum(t, 0, keepdims=True) for t in totals]
    return [jnp.concatenate([o[c] for o in out], 1) for c in range(2)]


def spread(errors, mask, hot, count):
    table = jnp.concatenate([mask[...] * e for e in errors], 0)
    out = lax.dot_general(
        pieces(table, count), hot[...], (((1,), (1,)), ((), ())), preferred_element_type=jnp.float32
    )
    return summed(out, count)


def folded(values):
    return sum(values[:, i : i + 128] for i in range(0, values.shape[1], 128))


def coefficients(mu):
    def inner(a, b, shift):
        total = None
        for i, x in enumerate(a):
            for j, y in enumerate(b):
                term = mu[i + j + shift]
                if x is not None:
                    term = x * term
                if y is not None:
                    term = y * term
                total = term if total is None else total + term
        return total

    residual, direction, field = [None], [None], []
    norm = mu[0]
    for step in range(ITERS):
        alpha = norm / inner(direction, direction, 1)
        along = [alpha if d is None else alpha * d for d in direction]
        field = [a if i >= len(field) else field[i] + a for i, a in enumerate(along)]
        residual = residual[:1] + [
            -a if i + 1 >= len(residual) else residual[i + 1] - a for i, a in enumerate(along)
        ]
        if step + 1 < ITERS:
            fresh = inner(residual, residual, 0)
            ratio = fresh / norm
            step_of = [ratio if d is None else ratio * d for d in direction]
            direction = [
                (1.0 if r is None else r) + (step_of[i] if i < len(step_of) else 0.0)
                for i, r in enumerate(residual)
            ]
            norm = fresh
    return field, residual


def kernel(
    ny,
    nz,
    nx,
    rhs_hbm,
    across_hbm,
    down_hbm,
    anchor_hbm,
    source_hbm,
    target_hbm,
    weight_hbm,
    count_hbm,
    basis_hbm,
    scalars,
    rhs_ref,
    across_ref,
    down_ref,
    anchor_ref,
    source_ref,
    target_ref,
    weight_ref,
    count_ref,
    hot_source,
    hot_target,
    mask_source,
    mask_left,
    mask_right,
    basis,
    slot_out,
    rim_out,
    halo_out,
    point_out,
    slot_in,
    rim_in,
    halo_in,
    point_in,
    sums,
    send_sem,
    recv_sem,
    load_sem,
    keep_sem,
    greet_sem,
):
    rows, cols = across_ref.shape[1:]
    slots = source_ref.shape[2]
    highs = cols // LOW
    bits_cols, bits_low = cols.bit_length() - 1, LOW.bit_length() - 1
    n_gz = ny * nz
    gz, xy = lax.axis_index("gz"), lax.axis_index("xy")
    y, z, x, core = gz // nz, gz % nz, xy // 2, xy % 2
    after, before = ((gz + 1) % n_gz, xy), ((gz + n_gz - 1) % n_gz, xy)
    below, above = (gz, (xy + 1) % nx), (gz, (xy + nx - 1) % nx)

    def peers(offsets):
        sizes = (ny, nz, nx // 2, 2)
        kept = []
        for offset in offsets:
            offset = tuple(o % n for o, n in zip(offset, sizes))
            if any(offset) and offset not in kept:
                kept.append(offset)
        return [
            (((y + o[0]) % ny) * nz + (z + o[1]) % nz, ((x + o[2]) % (nx // 2)) * 2 + (core + o[3]) % 2)
            for o in kept
        ]

    one_hop = peers(
        [(0, 1, 0, 0), (0, -1, 0, 0), (1, 0, 0, 0), (-1, 0, 0, 0), (0, 0, 1, 0), (0, 0, -1, 0), (0, 0, 0, 1)]
    )
    two_hops = peers([(0, 2, 0, 0), (0, -2, 0, 0), (2, 0, 0, 0), (0, 0, 2, 0)])
    four_hops = peers([(0, 4, 0, 0), (0, -4, 0, 0), (0, 0, 0, 1)])
    plane = [(j, 0, i, c) for j in range(ny) for i in range(nx // 2) for c in range(2)]
    line = [(0, i, 0, 0) for i in range(nz)]
    far_first = lambda o: -sum(min(d, n - d) for d, n in zip(o, (ny, nz, nx // 2, 2)))
    groups = [peers(sorted(plane, key=far_first)), peers(sorted(line, key=far_first))]

    barrier = pltpu.get_barrier_semaphore()
    met = [after, before, below, above] + one_hop
    for peer in met:
        pl.semaphore_signal(barrier, inc=1, device_id=peer, device_id_type=MESH)

    def greet(stage, who):
        for peer in who:
            pl.semaphore_signal(greet_sem.at[stage], inc=1, device_id=peer, device_id_type=MESH)

    loads = [
        pltpu.make_async_copy(src, dst, load_sem.at[i])
        for i, (src, dst) in enumerate(
            [
                (count_hbm, count_ref),
                (weight_hbm, weight_ref),
                (source_hbm, source_ref),
                (rhs_hbm, rhs_ref),
                (down_hbm, down_ref),
                (across_hbm, across_ref),
                (anchor_hbm, anchor_ref),
                (target_hbm, target_ref),
            ]
        )
    ]
    for load in loads:
        load.start()

    sent, kept = [], []

    def send(src, dst, peer, index):
        copy = pltpu.make_async_remote_copy(
            src_ref=src,
            dst_ref=dst,
            send_sem=send_sem.at[index],
            recv_sem=recv_sem.at[index],
            device_id=peer,
            device_id_type=MESH,
        )
        copy.start()
        sent.append(copy)
        return copy

    slot = lax.broadcasted_iota(jnp.int32, (1, slots), 1)
    loads[0].wait()
    loads[1].wait()
    live = ((slot < count_ref[0, 0] * BLOCK) & (gz < n_gz - 1)).astype(jnp.float32)
    for k in range(4):
        slot_out[k] = weight_ref[k, 0] * live
    loads[7].wait()
    slot_out[4] = target_ref[0].astype(jnp.float32)
    def post_halo(field, k):
        for c in range(2):
            halo_out[k, 0, c : c + 1, :] = field[c][:1]
            halo_out[k, 1, c : c + 1, :] = field[c][rows - 1 :]
        return [
            send(halo_out.at[k, 0], halo_in.at[k, 0], above, 2 + 4 * k),
            send(halo_out.at[k, 1], halo_in.at[k, 1], below, 3 + 4 * k),
        ]

    pl.semaphore_wait(barrier, len(met))
    copies = [
        send(slot_out, slot_in, after, 0),
    ]
    greet(0, one_hop)

    loads[3].wait()
    field = [rhs_ref[c, 0] for c in range(2)]
    halo = post_halo(field, 0)
    loads[4].wait()
    rim_out[...] = down_ref[0, rows - 1 :]
    copies.append(send(rim_out, rim_in, below, 1))

    low_id = lax.broadcasted_iota(jnp.int32, (LOW, slots), 0)
    place_id = lax.broadcasted_iota(jnp.int32, (highs * rows, slots), 0)

    def split(node):
        col = node & (cols - 1)
        return col & (LOW - 1), (col >> bits_low) * rows + (node >> bits_cols)

    loads[2].wait()
    low, place = split(source_ref[0])
    hot_source[...] = (low_id == low).astype(jnp.float32).astype(jnp.bfloat16)
    mask_source[...] = jnp.where(place_id == place, live, 0.0)


    loads[5].wait()
    loads[6].wait()
    across, down, anchor = across_ref[0], down_ref[0], anchor_ref[0]
    col_id = lax.broadcasted_iota(jnp.int32, (rows, cols), 1)
    row_id = lax.broadcasted_iota(jnp.int32, (rows, cols), 0)
    products = []

    for k in range(ITERS):
        base = 2 + 4 * k
        own = looked_up(pieces(stacked(field), 2), hot_source, [mask_source], 2)
        for c in range(2):
            point_out[k, 0, c : c + 1, :] = own[c]
        own_copy = send(point_out.at[k, 0], point_in.at[k, 0], after, base + 2)
        if k > 0:
            halo = post_halo(field, k)
        right = [jnp.where(col_id == cols - 1, 0.0, pltpu.roll(f, cols - 1, 1)) for f in field]
        if k == 0:
            copies[0].wait_recv()
            low, place = split(slot_in[4].astype(jnp.int32))
            hot_target[...] = (low_id == low).astype(jnp.float32).astype(jnp.bfloat16)
            for mask, one, two in ((mask_left, 0, 2), (mask_right, 1, 3)):
                mask[...] = jnp.where(
                    place_id == place,
                    slot_in[one],
                    jnp.where(place_id == place + 1, slot_in[two], 0.0),
                )
        table = jnp.concatenate([pieces(stacked(field), 2), pieces(stacked(right), 2)], 0)
        there = looked_up(table, hot_target, [mask_left, mask_right], 2)
        for c in range(2):
            point_out[k, 1, c : c + 1, :] = there[c]
        there_copy = send(point_out.at[k, 1], point_in.at[k, 1], before, base + 3)

        image, energy = [], None
        for c in range(2):
            f = field[c]
            gap = f - right[c]
            flux = across * gap
            fall = jnp.where(row_id == rows - 1, 0.0, f - pltpu.roll(f, rows - 1, 0))
            drop = down * fall
            held = anchor * f
            come = jnp.where(col_id == 0, 0.0, pltpu.roll(flux, 1, 1))
            above_me = jnp.where(row_id == 0, 0.0, pltpu.roll(drop, 1, 0))
            image.append(flux - come + drop - above_me + held)
            if k == ITERS - 1:
                term = flux * gap + drop * fall + held * f
                energy = term if energy is None else energy + term
        if k > 0:
            products.append(sum(folded(a * b) for a, b in zip(former, field)))
        products.append(sum(folded(a * a) for a in field))
        if k == ITERS - 1:
            rows_known = [jnp.sum(p, 0, keepdims=True) for p in products]
            energy = folded(energy)

        if k == 0:
            pl.semaphore_wait(greet_sem.at[0], len(one_hop))
            greet(1, two_hops)
        if k == 1:
            pl.semaphore_wait(greet_sem.at[1], len(two_hops))
            greet(2, four_hops)

        def onward():
            own_copy.wait_recv()
            error_in = [there[c] - point_in[k, 0, c : c + 1, :] for c in range(2)]
            left = unstacked(spread(error_in, mask_left, hot_target, 2), rows, highs)
            more = unstacked(spread(error_in, mask_right, hot_target, 2), rows, highs)
            return [a + pltpu.roll(b, 1, 1) for a, b in zip(left, more)]

        if k < ITERS - 1:
            image = [a + b for a, b in zip(image, onward())]

        if k == 0:
            copies[1].wait_recv()
        halo[0].wait_recv()
        halo[1].wait_recv()
        rim = jnp.where(xy > 0, rim_in[...], 0.0)
        for c in range(2):
            f = field[c]
            upper = halo_in[k, 1, c : c + 1, :]
            lower = jnp.where(xy < nx - 1, halo_in[k, 0, c : c + 1, :], 0.0)
            fall = f - lower
            drop = down * fall
            edge = jnp.where(row_id == 0, rim * (f - upper), 0.0)
            image[c] = image[c] + jnp.where(row_id == rows - 1, drop + edge, edge)
            if k == ITERS - 1:
                energy = energy + folded(jnp.where(row_id == rows - 1, drop * fall, 0.0))

        there_copy.wait_recv()
        error = [point_in[k, 1, c : c + 1, :] - own[c] for c in range(2)]
        if k == ITERS - 1:
            tie = sum(e * e for e in error)
            last = jnp.sum(energy, 0, keepdims=True) + folded(tie)
            rows_known.append(last * (1.0 / SCALE))
            rows_known.append(jnp.zeros((8 - MOMENTS, 128), jnp.float32))
            lanes = jnp.concatenate(rows_known, 0)
            eight = lax.broadcasted_iota(jnp.int32, (8, 128), 0)
            total = jnp.sum(lanes, 1, keepdims=True)
            lane = lax.broadcasted_iota(jnp.int32, (8, 128), 1)
            total = jnp.sum(jnp.where(lane == eight, total, 0.0), 0, keepdims=True)

        def post_sum(stage, total):
            sums[stage, 0] = total
            if stage == 0:
                pl.semaphore_wait(greet_sem.at[2], len(four_hops))
            index = 2 + 4 * ITERS + stage
            for i, peer in enumerate(groups[stage]):
                copy = pltpu.make_async_remote_copy(
                    src_ref=sums.at[stage, 0],
                    dst_ref=sums.at[stage, i + 1],
                    send_sem=send_sem.at[index],
                    recv_sem=recv_sem.at[index],
                    device_id=peer,
                    device_id_type=MESH,
                )
                copy.start()

        def take_sum(stage):
            index = 2 + 4 * ITERS + stage
            count = len(groups[stage])
            arrived = sums.at[stage, pl.ds(1, count)]
            pltpu.make_async_copy(arrived, arrived, recv_sem.at[index]).wait()
            return functools.reduce(lambda a, b: a + b, [sums[stage, i] for i in range(count + 1)])

        if k == ITERS - 1:
            post_sum(0, total)
            image = [a + b for a, b in zip(image, onward())]
        back = unstacked(spread(error, mask_source, hot_source, 2), rows, highs)
        latest = [(a - b) * (1.0 / SCALE) for a, b in zip(image, back)]
        for c in range(2):
            basis[k, c] = latest[c]
        keep = pltpu.make_async_copy(basis.at[k], basis_hbm.at[k], keep_sem.at[k])
        keep.start()
        kept.append(keep)
        former, field = field, latest

    post_sum(1, take_sum(0))
    total = take_sum(1)
    lane = lax.broadcasted_iota(jnp.int32, (1, 128), 1)
    mu = [
        jnp.sum(jnp.where(lane == i, total, 0.0), 1, keepdims=True) for i in range(MOMENTS)
    ]
    steps, rest = coefficients(mu)
    rows_of = [jnp.broadcast_to(s, (1, 128)) for s in [s * (1.0 / SCALE) for s in steps] + rest[1:]]
    scalars[...] = jnp.concatenate(rows_of + [jnp.zeros((8 - 2 * ITERS, 128), jnp.float32)], 0)

    for keep in kept:
        keep.wait()
    for copy in sent:
        copy.wait_send()
    for stage in range(2):
        count = len(groups[stage])
        gone = sums.at[stage, pl.ds(1, count)]
        pltpu.make_async_copy(gone, gone, send_sem.at[2 + 4 * ITERS + stage]).wait()


def combine(rhs_hbm, basis_hbm, scalars_hbm, x_hbm, r_hbm, rhs, basis, scalars, x, r, load_sem, save_sem):
    loads = [
        pltpu.make_async_copy(src, dst, load_sem.at[i])
        for i, (src, dst) in enumerate(
            [(scalars_hbm, scalars)]
            + [
                pair
                for c in range(2)
                for pair in ((rhs_hbm.at[c], rhs.at[c]), (basis_hbm.at[:, c], basis.at[:, c]))
            ]
        )
    ]
    for load in loads:
        load.start()
    loads[0].wait()
    values = [scalars[i : i + 1, :1] for i in range(2 * ITERS)]
    saves = []
    for c in range(2):
        loads[1 + 2 * c].wait()
        loads[2 + 2 * c].wait()
        powers = [rhs[c, 0]] + [basis[i, c] for i in range(ITERS)]
        x[c, 0] = sum(s * v for s, v in zip(values[:ITERS], powers))
        r[c, 0] = powers[0] + sum(s * v for s, v in zip(values[ITERS:], powers[1:]))
        for n, (src, dst) in enumerate(((x, x_hbm), (r, r_hbm))):
            save = pltpu.make_async_copy(src.at[c], dst.at[c], save_sem.at[2 * c + n])
            save.start()
            saves.append(save)
    for save in saves:
        save.wait()


def body(nz, rhs, across, down, anchor, source, target, weight, count):
    n_gz, nx = lax.axis_size("gz"), lax.axis_size("xy")
    ny = n_gz // nz
    rows, cols = across.shape[1:]
    slots = source.shape[2]
    places = rows * cols // LOW
    f32, bf16 = jnp.float32, jnp.bfloat16
    vmem = pl.BlockSpec(memory_space=pltpu.VMEM)
    hbm = pl.BlockSpec(memory_space=pltpu.HBM)
    args = (rhs, across, down, anchor, source, target, weight, count)
    copies = 2 + 4 * ITERS + 2
    widest = max(nx * ny, nz)
    basis, scalars = pl.pallas_call(
        functools.partial(kernel, ny, nz, nx),
        out_shape=(
            jax.ShapeDtypeStruct((ITERS, 2, rows, cols), f32),
            jax.ShapeDtypeStruct((8, 128), f32),
        ),
        in_specs=[hbm] * len(args),
        out_specs=(hbm, vmem),
        scratch_shapes=[
            pltpu.VMEM(rhs.shape, f32),
            pltpu.VMEM(across.shape, f32),
            pltpu.VMEM(down.shape, f32),
            pltpu.VMEM(anchor.shape, f32),
            pltpu.VMEM(source.shape, jnp.int32),
            pltpu.VMEM(target.shape, jnp.int32),
            pltpu.VMEM(weight.shape, f32),
            pltpu.SMEM(count.shape, jnp.int32),
            pltpu.VMEM((LOW, slots), bf16),
            pltpu.VMEM((LOW, slots), bf16),
            pltpu.VMEM((places, slots), f32),
            pltpu.VMEM((places, slots), f32),
            pltpu.VMEM((places, slots), f32),
            pltpu.VMEM((ITERS, 2, rows, cols), f32),
            pltpu.VMEM((5, 1, slots), f32),
            pltpu.VMEM((1, cols), f32),
            pltpu.VMEM((ITERS, 2, 2, cols), f32),
            pltpu.VMEM((ITERS, 2, 2, slots), f32),
            pltpu.VMEM((5, 1, slots), f32),
            pltpu.VMEM((1, cols), f32),
            pltpu.VMEM((ITERS, 2, 2, cols), f32),
            pltpu.VMEM((ITERS, 2, 2, slots), f32),
            pltpu.VMEM((2, widest, 1, 128), f32),
            pltpu.SemaphoreType.DMA((copies,)),
            pltpu.SemaphoreType.DMA((copies,)),
            pltpu.SemaphoreType.DMA((8,)),
            pltpu.SemaphoreType.DMA((ITERS,)),
            pltpu.SemaphoreType.REGULAR((3,)),
        ],
        compiler_params=pltpu.CompilerParams(
            collective_id=0, has_side_effects=True, vmem_limit_bytes=63 * 1024 * 1024
        ),
    )(*args)
    out = jax.ShapeDtypeStruct(rhs.shape, f32)
    return pl.pallas_call(
        combine,
        out_shape=(out, out),
        in_specs=[hbm] * 3,
        out_specs=(hbm, hbm),
        scratch_shapes=[
            pltpu.VMEM(rhs.shape, f32),
            pltpu.VMEM(basis.shape, f32),
            pltpu.VMEM(scalars.shape, f32),
            pltpu.VMEM(rhs.shape, f32),
            pltpu.VMEM(rhs.shape, f32),
            pltpu.SemaphoreType.DMA((5,)),
            pltpu.SemaphoreType.DMA((4,)),
        ],
        compiler_params=pltpu.CompilerParams(vmem_limit_bytes=63 * 1024 * 1024),
    )(rhs, basis, scalars)


def solution(mesh, nz=16):
    in_specs = (
        P(None, "gz", "xy", None),
        P("gz", "xy", None),
        P("gz", "xy", None),
        P("gz", "xy", None),
        P("gz", "xy", None),
        P("gz", "xy", None),
        P(None, "gz", "xy", None),
        P("gz", "xy"),
    )
    out_specs = (P(None, "gz", "xy", None), P(None, "gz", "xy", None))
    return jax.shard_map(
        functools.partial(body, nz), mesh=mesh, in_specs=in_specs, out_specs=out_specs, check_vma=False
    )
```

```python
import functools

import jax
import jax.numpy as jnp
from jax import lax
from jax.experimental import pallas as pl
from jax.experimental.pallas import tpu as pltpu
from jax.sharding import PartitionSpec as P

BLOCK = 128
ITERS = 3
LOW = 256
SCALE = 8.0
MESH = pl.DeviceIdType.MESH
MOMENTS = 2 * ITERS


def pieces(values, count):
    out = []
    for i in range(count):
        part = values.astype(jnp.bfloat16)
        out.append(part)
        if i + 1 < count:
            values = values - part.astype(jnp.float32)
    return jnp.concatenate(out, 0)


def summed(pieces_of, count):
    rows = pieces_of.shape[0] // count
    total = pieces_of[:rows]
    for i in range(1, count):
        total = total + pieces_of[i * rows : (i + 1) * rows]
    return total


def stacked(field):
    return jnp.concatenate(
        [part[:, h : h + LOW] for part in field for h in range(0, part.shape[1], LOW)], 0
    )


def unstacked(table, rows, highs):
    return [
        jnp.concatenate(
            [table[(c * highs + h) * rows : (c * highs + h + 1) * rows] for h in range(highs)], 1
        )
        for c in range(2)
    ]


def looked_up(table, hot, masks, first):
    wide = hot.shape[1]
    cut = min(wide, 256)
    out = []
    for j in range(0, wide, cut):
        found = jnp.dot(table, hot[:, j : j + cut], preferred_element_type=jnp.float32)
        out.append([])
        per = found.shape[0] // len(masks)
        totals = None
        for m, mask in enumerate(masks):
            got = summed(found[m * per : (m + 1) * per], first)
            half = got.shape[0] // 2
            terms = [got[c * half : (c + 1) * half] * mask[:, j : j + cut] for c in range(2)]
            totals = terms if totals is None else [a + b for a, b in zip(totals, terms)]
        out[-1] = [jnp.sum(t, 0, keepdims=True) for t in totals]
    return [jnp.concatenate([o[c] for o in out], 1) for c in range(2)]


def spread(errors, mask, hot, count):
    table = jnp.concatenate([mask[...] * e for e in errors], 0)
    out = lax.dot_general(
        pieces(table, count), hot[...], (((1,), (1,)), ((), ())), preferred_element_type=jnp.float32
    )
    return summed(out, count)


def folded(values):
    return sum(values[:, i : i + 128] for i in range(0, values.shape[1], 128))


def coefficients(mu):
    def inner(a, b, shift):
        total = None
        for i, x in enumerate(a):
            for j, y in enumerate(b):
                term = mu[i + j + shift]
                if x is not None:
                    term = x * term
                if y is not None:
                    term = y * term
                total = term if total is None else total + term
        return total

    residual, direction, field = [None], [None], []
    norm = mu[0]
    for step in range(ITERS):
        alpha = norm / inner(direction, direction, 1)
        along = [alpha if d is None else alpha * d for d in direction]
        field = [a if i >= len(field) else field[i] + a for i, a in enumerate(along)]
        residual = residual[:1] + [
            -a if i + 1 >= len(residual) else residual[i + 1] - a for i, a in enumerate(along)
        ]
        if step + 1 < ITERS:
            fresh = inner(residual, residual, 0)
            ratio = fresh / norm
            step_of = [ratio if d is None else ratio * d for d in direction]
            direction = [
                (1.0 if r is None else r) + (step_of[i] if i < len(step_of) else 0.0)
                for i, r in enumerate(residual)
            ]
            norm = fresh
    return field, residual


def kernel(
    ny,
    nz,
    nx,
    rhs_hbm,
    across_hbm,
    down_hbm,
    anchor_hbm,
    source_hbm,
    target_hbm,
    weight_hbm,
    count_hbm,
    basis_hbm,
    scalars,
    rhs_ref,
    across_ref,
    down_ref,
    anchor_ref,
    source_ref,
    target_ref,
    weight_ref,
    count_ref,
    hot_source,
    hot_target,
    mask_source,
    mask_target,
    basis,
    slot_out,
    rim_out,
    halo_out,
    point_out,
    slot_in,
    rim_in,
    halo_in,
    point_in,
    sums,
    send_sem,
    recv_sem,
    load_sem,
    keep_sem,
    greet_sem,
):
    rows, cols = across_ref.shape[1:]
    slots = source_ref.shape[2]
    highs = cols // LOW
    bits_cols, bits_low = cols.bit_length() - 1, LOW.bit_length() - 1
    n_gz = ny * nz
    gz, xy = lax.axis_index("gz"), lax.axis_index("xy")
    y, z, x, core = gz // nz, gz % nz, xy // 2, xy % 2
    after, before = ((gz + 1) % n_gz, xy), ((gz + n_gz - 1) % n_gz, xy)
    below, above = (gz, (xy + 1) % nx), (gz, (xy + nx - 1) % nx)

    def peers(offsets):
        sizes = (ny, nz, nx // 2, 2)
        kept = []
        for offset in offsets:
            offset = tuple(o % n for o, n in zip(offset, sizes))
            if any(offset) and offset not in kept:
                kept.append(offset)
        return [
            (((y + o[0]) % ny) * nz + (z + o[1]) % nz, ((x + o[2]) % (nx // 2)) * 2 + (core + o[3]) % 2)
            for o in kept
        ]

    one_hop = peers(
        [(0, 1, 0, 0), (0, -1, 0, 0), (1, 0, 0, 0), (-1, 0, 0, 0), (0, 0, 1, 0), (0, 0, -1, 0), (0, 0, 0, 1)]
    )
    two_hops = peers([(0, 2, 0, 0), (0, -2, 0, 0), (2, 0, 0, 0), (0, 0, 2, 0)])
    four_hops = peers([(0, 4, 0, 0), (0, -4, 0, 0), (0, 0, 0, 1)])
    plane = [(j, 0, i, c) for j in range(ny) for i in range(nx // 2) for c in range(2)]
    line = [(0, i, 0, 0) for i in range(nz)]
    far_first = lambda o: -sum(min(d, n - d) for d, n in zip(o, (ny, nz, nx // 2, 2)))
    groups = [peers(sorted(plane, key=far_first)), peers(sorted(line, key=far_first))]

    barrier = pltpu.get_barrier_semaphore()
    met = [after, before, below, above] + one_hop
    for peer in met:
        pl.semaphore_signal(barrier, inc=1, device_id=peer, device_id_type=MESH)

    def greet(stage, who):
        for peer in who:
            pl.semaphore_signal(greet_sem.at[stage], inc=1, device_id=peer, device_id_type=MESH)

    loads = [
        pltpu.make_async_copy(src, dst, load_sem.at[i])
        for i, (src, dst) in enumerate(
            [
                (count_hbm, count_ref),
                (weight_hbm, weight_ref),
                (source_hbm, source_ref),
                (rhs_hbm, rhs_ref),
                (down_hbm, down_ref),
                (across_hbm, across_ref),
                (anchor_hbm, anchor_ref),
                (target_hbm, target_ref),
            ]
        )
    ]
    for load in loads:
        load.start()

    sent, kept = [], []

    def send(src, dst, peer, index):
        copy = pltpu.make_async_remote_copy(
            src_ref=src,
            dst_ref=dst,
            send_sem=send_sem.at[index],
            recv_sem=recv_sem.at[index],
            device_id=peer,
            device_id_type=MESH,
        )
        copy.start()
        sent.append(copy)
        return copy

    slot = lax.broadcasted_iota(jnp.int32, (1, slots), 1)
    loads[0].wait()
    loads[1].wait()
    live = ((slot < count_ref[0, 0] * BLOCK) & (gz < n_gz - 1)).astype(jnp.float32)
    for k in range(4):
        slot_out[k] = weight_ref[k, 0] * live
    loads[7].wait()
    slot_out[4] = target_ref[0].astype(jnp.float32)
    def post_halo(field, k):
        for c in range(2):
            halo_out[k, 0, c : c + 1, :] = field[c][:1]
            halo_out[k, 1, c : c + 1, :] = field[c][rows - 1 :]
        return [
            send(halo_out.at[k, 0], halo_in.at[k, 0], above, 2 + 4 * k),
            send(halo_out.at[k, 1], halo_in.at[k, 1], below, 3 + 4 * k),
        ]

    pl.semaphore_wait(barrier, len(met))
    copies = [
        send(slot_out, slot_in, after, 0),
    ]
    greet(0, one_hop)

    loads[3].wait()
    field = [rhs_ref[c, 0] for c in range(2)]
    halo = post_halo(field, 0)
    loads[4].wait()
    rim_out[...] = down_ref[0, rows - 1 :]
    copies.append(send(rim_out, rim_in, below, 1))

    low_id = lax.broadcasted_iota(jnp.int32, (LOW, slots), 0)
    place_id = lax.broadcasted_iota(jnp.int32, (highs * rows, slots), 0)

    def split(node):
        col = node & (cols - 1)
        return col & (LOW - 1), (col >> bits_low) * rows + (node >> bits_cols)

    loads[2].wait()
    low, place = split(source_ref[0])
    hot_source[...] = (low_id == low).astype(jnp.float32).astype(jnp.bfloat16)
    mask_source[...] = jnp.where(place_id == place, live, 0.0)


    loads[5].wait()
    loads[6].wait()
    across, down, anchor = across_ref[0], down_ref[0], anchor_ref[0]
    col_id = lax.broadcasted_iota(jnp.int32, (rows, cols), 1)
    row_id = lax.broadcasted_iota(jnp.int32, (rows, cols), 0)
    products = []

    for k in range(ITERS):
        base = 2 + 4 * k
        table = pieces(stacked(field), 2)
        own = looked_up(table, hot_source, [mask_source], 2)
        for c in range(2):
            point_out[k, 0, c : c + 1, :] = own[c]
        own_copy = send(point_out.at[k, 0], point_in.at[k, 0], after, base + 2)
        if k > 0:
            halo = post_halo(field, k)
        if k == 0:
            copies[0].wait_recv()
            node = slot_in[4].astype(jnp.int32)
            for side in range(2):
                low, place = split(node + side)
                half = slice(side * slots, (side + 1) * slots)
                hot_target[:, half] = (low_id == low).astype(jnp.float32).astype(jnp.bfloat16)
                mask_target[:, half] = jnp.where(
                    place_id == place,
                    slot_in[side],
                    jnp.where(place_id == place + 1, slot_in[2 + side], 0.0),
                )
        both = looked_up(table, hot_target, [mask_target], 2)
        there = [b[:, :slots] + b[:, slots:] for b in both]
        for c in range(2):
            point_out[k, 1, c : c + 1, :] = there[c]
        there_copy = send(point_out.at[k, 1], point_in.at[k, 1], before, base + 3)

        right = [jnp.where(col_id == cols - 1, 0.0, pltpu.roll(f, cols - 1, 1)) for f in field]
        image, energy = [], None
        for c in range(2):
            f = field[c]
            gap = f - right[c]
            flux = across * gap
            fall = jnp.where(row_id == rows - 1, 0.0, f - pltpu.roll(f, rows - 1, 0))
            drop = down * fall
            held = anchor * f
            come = jnp.where(col_id == 0, 0.0, pltpu.roll(flux, 1, 1))
            above_me = jnp.where(row_id == 0, 0.0, pltpu.roll(drop, 1, 0))
            image.append(flux - come + drop - above_me + held)
            if k == ITERS - 1:
                term = flux * gap + drop * fall + held * f
                energy = term if energy is None else energy + term
        if k > 0:
            products.append(sum(folded(a * b) for a, b in zip(former, field)))
        products.append(sum(folded(a * a) for a in field))
        if k == ITERS - 1:
            rows_known = [jnp.sum(p, 0, keepdims=True) for p in products]
            energy = folded(energy)

        if k == 0:
            pl.semaphore_wait(greet_sem.at[0], len(one_hop))
            greet(1, two_hops)
        if k == 1:
            pl.semaphore_wait(greet_sem.at[1], len(two_hops))
            greet(2, four_hops)

        def onward():
            own_copy.wait_recv()
            error_in = [there[c] - point_in[k, 0, c : c + 1, :] for c in range(2)]
            twice = [jnp.concatenate([e, e], 1) for e in error_in]
            return unstacked(spread(twice, mask_target, hot_target, 2), rows, highs)

        if k < ITERS - 1:
            image = [a + b for a, b in zip(image, onward())]

        if k == 0:
            copies[1].wait_recv()
        halo[0].wait_recv()
        halo[1].wait_recv()
        rim = jnp.where(xy > 0, rim_in[...], 0.0)
        for c in range(2):
            f = field[c]
            upper = halo_in[k, 1, c : c + 1, :]
            lower = jnp.where(xy < nx - 1, halo_in[k, 0, c : c + 1, :], 0.0)
            fall = f - lower
            drop = down * fall
            edge = jnp.where(row_id == 0, rim * (f - upper), 0.0)
            image[c] = image[c] + jnp.where(row_id == rows - 1, drop + edge, edge)
            if k == ITERS - 1:
                energy = energy + folded(jnp.where(row_id == rows - 1, drop * fall, 0.0))

        there_copy.wait_recv()
        error = [point_in[k, 1, c : c + 1, :] - own[c] for c in range(2)]
        if k == ITERS - 1:
            tie = sum(e * e for e in error)
            last = jnp.sum(energy, 0, keepdims=True) + folded(tie)
            rows_known.append(last * (1.0 / SCALE))
            rows_known.append(jnp.zeros((8 - MOMENTS, 128), jnp.float32))
            lanes = jnp.concatenate(rows_known, 0)
            eight = lax.broadcasted_iota(jnp.int32, (8, 128), 0)
            total = jnp.sum(lanes, 1, keepdims=True)
            lane = lax.broadcasted_iota(jnp.int32, (8, 128), 1)
            total = jnp.sum(jnp.where(lane == eight, total, 0.0), 0, keepdims=True)

        def post_sum(stage, total):
            sums[stage, 0] = total
            if stage == 0:
                pl.semaphore_wait(greet_sem.at[2], len(four_hops))
            index = 2 + 4 * ITERS + stage
            for i, peer in enumerate(groups[stage]):
                copy = pltpu.make_async_remote_copy(
                    src_ref=sums.at[stage, 0],
                    dst_ref=sums.at[stage, i + 1],
                    send_sem=send_sem.at[index],
                    recv_sem=recv_sem.at[index],
                    device_id=peer,
                    device_id_type=MESH,
                )
                copy.start()

        def take_sum(stage):
            index = 2 + 4 * ITERS + stage
            count = len(groups[stage])
            arrived = sums.at[stage, pl.ds(1, count)]
            pltpu.make_async_copy(arrived, arrived, recv_sem.at[index]).wait()
            return functools.reduce(lambda a, b: a + b, [sums[stage, i] for i in range(count + 1)])

        if k == ITERS - 1:
            post_sum(0, total)
            image = [a + b for a, b in zip(image, onward())]
        back = unstacked(spread(error, mask_source, hot_source, 2), rows, highs)
        latest = [(a - b) * (1.0 / SCALE) for a, b in zip(image, back)]
        for c in range(2):
            basis[k, c] = latest[c]
        keep = pltpu.make_async_copy(basis.at[k], basis_hbm.at[k], keep_sem.at[k])
        keep.start()
        kept.append(keep)
        former, field = field, latest

    post_sum(1, take_sum(0))
    total = take_sum(1)
    lane = lax.broadcasted_iota(jnp.int32, (1, 128), 1)
    mu = [
        jnp.sum(jnp.where(lane == i, total, 0.0), 1, keepdims=True) for i in range(MOMENTS)
    ]
    steps, rest = coefficients(mu)
    rows_of = [jnp.broadcast_to(s, (1, 128)) for s in [s * (1.0 / SCALE) for s in steps] + rest[1:]]
    scalars[...] = jnp.concatenate(rows_of + [jnp.zeros((8 - 2 * ITERS, 128), jnp.float32)], 0)

    for keep in kept:
        keep.wait()
    for copy in sent:
        copy.wait_send()
    for stage in range(2):
        count = len(groups[stage])
        gone = sums.at[stage, pl.ds(1, count)]
        pltpu.make_async_copy(gone, gone, send_sem.at[2 + 4 * ITERS + stage]).wait()


def combine(rhs_hbm, basis_hbm, scalars_hbm, x_hbm, r_hbm, rhs, basis, scalars, x, r, load_sem, save_sem):
    loads = [
        pltpu.make_async_copy(src, dst, load_sem.at[i])
        for i, (src, dst) in enumerate(
            [(scalars_hbm, scalars)]
            + [
                pair
                for c in range(2)
                for pair in ((rhs_hbm.at[c], rhs.at[c]), (basis_hbm.at[:, c], basis.at[:, c]))
            ]
        )
    ]
    for load in loads:
        load.start()
    loads[0].wait()
    values = [scalars[i : i + 1, :1] for i in range(2 * ITERS)]
    saves = []
    for c in range(2):
        loads[1 + 2 * c].wait()
        loads[2 + 2 * c].wait()
        powers = [rhs[c, 0]] + [basis[i, c] for i in range(ITERS)]
        x[c, 0] = sum(s * v for s, v in zip(values[:ITERS], powers))
        r[c, 0] = powers[0] + sum(s * v for s, v in zip(values[ITERS:], powers[1:]))
        for n, (src, dst) in enumerate(((x, x_hbm), (r, r_hbm))):
            save = pltpu.make_async_copy(src.at[c], dst.at[c], save_sem.at[2 * c + n])
            save.start()
            saves.append(save)
    for save in saves:
        save.wait()


def body(nz, rhs, across, down, anchor, source, target, weight, count):
    n_gz, nx = lax.axis_size("gz"), lax.axis_size("xy")
    ny = n_gz // nz
    rows, cols = across.shape[1:]
    slots = source.shape[2]
    places = rows * cols // LOW
    f32, bf16 = jnp.float32, jnp.bfloat16
    vmem = pl.BlockSpec(memory_space=pltpu.VMEM)
    hbm = pl.BlockSpec(memory_space=pltpu.HBM)
    args = (rhs, across, down, anchor, source, target, weight, count)
    copies = 2 + 4 * ITERS + 2
    widest = max(nx * ny, nz)
    basis, scalars = pl.pallas_call(
        functools.partial(kernel, ny, nz, nx),
        out_shape=(
            jax.ShapeDtypeStruct((ITERS, 2, rows, cols), f32),
            jax.ShapeDtypeStruct((8, 128), f32),
        ),
        in_specs=[hbm] * len(args),
        out_specs=(hbm, vmem),
        scratch_shapes=[
            pltpu.VMEM(rhs.shape, f32),
            pltpu.VMEM(across.shape, f32),
            pltpu.VMEM(down.shape, f32),
            pltpu.VMEM(anchor.shape, f32),
            pltpu.VMEM(source.shape, jnp.int32),
            pltpu.VMEM(target.shape, jnp.int32),
            pltpu.VMEM(weight.shape, f32),
            pltpu.SMEM(count.shape, jnp.int32),
            pltpu.VMEM((LOW, slots), bf16),
            pltpu.VMEM((LOW, 2 * slots), bf16),
            pltpu.VMEM((places, slots), f32),
            pltpu.VMEM((places, 2 * slots), f32),
            pltpu.VMEM((ITERS, 2, rows, cols), f32),
            pltpu.VMEM((5, 1, slots), f32),
            pltpu.VMEM((1, cols), f32),
            pltpu.VMEM((ITERS, 2, 2, cols), f32),
            pltpu.VMEM((ITERS, 2, 2, slots), f32),
            pltpu.VMEM((5, 1, slots), f32),
            pltpu.VMEM((1, cols), f32),
            pltpu.VMEM((ITERS, 2, 2, cols), f32),
            pltpu.VMEM((ITERS, 2, 2, slots), f32),
            pltpu.VMEM((2, widest, 1, 128), f32),
            pltpu.SemaphoreType.DMA((copies,)),
            pltpu.SemaphoreType.DMA((copies,)),
            pltpu.SemaphoreType.DMA((8,)),
            pltpu.SemaphoreType.DMA((ITERS,)),
            pltpu.SemaphoreType.REGULAR((3,)),
        ],
        compiler_params=pltpu.CompilerParams(
            collective_id=0, has_side_effects=True, vmem_limit_bytes=63 * 1024 * 1024
        ),
    )(*args)
    out = jax.ShapeDtypeStruct(rhs.shape, f32)
    return pl.pallas_call(
        combine,
        out_shape=(out, out),
        in_specs=[hbm] * 3,
        out_specs=(hbm, hbm),
        scratch_shapes=[
            pltpu.VMEM(rhs.shape, f32),
            pltpu.VMEM(basis.shape, f32),
            pltpu.VMEM(scalars.shape, f32),
            pltpu.VMEM(rhs.shape, f32),
            pltpu.VMEM(rhs.shape, f32),
            pltpu.SemaphoreType.DMA((5,)),
            pltpu.SemaphoreType.DMA((4,)),
        ],
        compiler_params=pltpu.CompilerParams(vmem_limit_bytes=63 * 1024 * 1024),
    )(rhs, basis, scalars)


def solution(mesh, nz=16):
    in_specs = (
        P(None, "gz", "xy", None),
        P("gz", "xy", None),
        P("gz", "xy", None),
        P("gz", "xy", None),
        P("gz", "xy", None),
        P("gz", "xy", None),
        P(None, "gz", "xy", None),
        P("gz", "xy"),
    )
    out_specs = (P(None, "gz", "xy", None), P(None, "gz", "xy", None))
    return jax.shard_map(
        functools.partial(body, nz), mesh=mesh, in_specs=in_specs, out_specs=out_specs, check_vma=False
    )
```

```python
import functools

import jax
import jax.numpy as jnp
from jax import lax
from jax.experimental import pallas as pl
from jax.experimental.pallas import tpu as pltpu
from jax.sharding import PartitionSpec as P

BLOCK = 128
ITERS = 3
LOW = 256
SCALE = 8.0
MESH = pl.DeviceIdType.MESH
MOMENTS = 2 * ITERS


def pieces(values, count):
    out = []
    for i in range(count):
        part = values.astype(jnp.bfloat16)
        out.append(part)
        if i + 1 < count:
            values = values - part.astype(jnp.float32)
    return jnp.concatenate(out, 0)


def summed(pieces_of, count):
    rows = pieces_of.shape[0] // count
    total = pieces_of[:rows]
    for i in range(1, count):
        total = total + pieces_of[i * rows : (i + 1) * rows]
    return total


def stacked(field):
    return jnp.concatenate(
        [part[:, h : h + LOW] for part in field for h in range(0, part.shape[1], LOW)], 0
    )


def unstacked(table, rows, highs):
    return [
        jnp.concatenate(
            [table[(c * highs + h) * rows : (c * highs + h + 1) * rows] for h in range(highs)], 1
        )
        for c in range(2)
    ]


def looked_up(table, hot, masks, first):
    wide = hot.shape[1]
    cut = min(wide, 256)
    out = []
    for j in range(0, wide, cut):
        found = jnp.dot(table, hot[:, j : j + cut], preferred_element_type=jnp.float32)
        out.append([])
        per = found.shape[0] // len(masks)
        totals = None
        for m, mask in enumerate(masks):
            got = summed(found[m * per : (m + 1) * per], first)
            half = got.shape[0] // 2
            terms = [got[c * half : (c + 1) * half] * mask[:, j : j + cut] for c in range(2)]
            totals = terms if totals is None else [a + b for a, b in zip(totals, terms)]
        out[-1] = [jnp.sum(t, 0, keepdims=True) for t in totals]
    return [jnp.concatenate([o[c] for o in out], 1) for c in range(2)]


def spread(errors, mask, hot, count):
    table = jnp.concatenate([mask[...] * e for e in errors], 0)
    out = lax.dot_general(
        pieces(table, count), hot[...], (((1,), (1,)), ((), ())), preferred_element_type=jnp.float32
    )
    return summed(out, count)


def folded(values):
    return sum(values[:, i : i + 128] for i in range(0, values.shape[1], 128))


def coefficients(mu):
    def inner(a, b, shift):
        total = None
        for i, x in enumerate(a):
            for j, y in enumerate(b):
                term = mu[i + j + shift]
                if x is not None:
                    term = x * term
                if y is not None:
                    term = y * term
                total = term if total is None else total + term
        return total

    residual, direction, field = [None], [None], []
    norm = mu[0]
    for step in range(ITERS):
        alpha = norm / inner(direction, direction, 1)
        along = [alpha if d is None else alpha * d for d in direction]
        field = [a if i >= len(field) else field[i] + a for i, a in enumerate(along)]
        residual = residual[:1] + [
            -a if i + 1 >= len(residual) else residual[i + 1] - a for i, a in enumerate(along)
        ]
        if step + 1 < ITERS:
            fresh = inner(residual, residual, 0)
            ratio = fresh / norm
            step_of = [ratio if d is None else ratio * d for d in direction]
            direction = [
                (1.0 if r is None else r) + (step_of[i] if i < len(step_of) else 0.0)
                for i, r in enumerate(residual)
            ]
            norm = fresh
    return field, residual


def kernel(
    ny,
    nz,
    nx,
    rhs_hbm,
    across_hbm,
    down_hbm,
    anchor_hbm,
    source_hbm,
    target_hbm,
    weight_hbm,
    count_hbm,
    basis_hbm,
    scalars,
    rhs_ref,
    across_ref,
    down_ref,
    anchor_ref,
    source_ref,
    target_ref,
    weight_ref,
    count_ref,
    hot_source,
    hot_target,
    mask_source,
    mask_left,
    mask_right,
    basis,
    slot_out,
    rim_out,
    halo_out,
    point_out,
    slot_in,
    rim_in,
    halo_in,
    point_in,
    sums,
    send_sem,
    recv_sem,
    load_sem,
    keep_sem,
    greet_sem,
):
    rows, cols = across_ref.shape[1:]
    slots = source_ref.shape[2]
    highs = cols // LOW
    bits_cols, bits_low = cols.bit_length() - 1, LOW.bit_length() - 1
    n_gz = ny * nz
    gz, xy = lax.axis_index("gz"), lax.axis_index("xy")
    y, z, x, core = gz // nz, gz % nz, xy // 2, xy % 2
    after, before = ((gz + 1) % n_gz, xy), ((gz + n_gz - 1) % n_gz, xy)
    below, above = (gz, (xy + 1) % nx), (gz, (xy + nx - 1) % nx)

    def peers(offsets):
        sizes = (ny, nz, nx // 2, 2)
        kept = []
        for offset in offsets:
            offset = tuple(o % n for o, n in zip(offset, sizes))
            if any(offset) and offset not in kept:
                kept.append(offset)
        return [
            (((y + o[0]) % ny) * nz + (z + o[1]) % nz, ((x + o[2]) % (nx // 2)) * 2 + (core + o[3]) % 2)
            for o in kept
        ]

    one_hop = peers(
        [(0, 1, 0, 0), (0, -1, 0, 0), (1, 0, 0, 0), (-1, 0, 0, 0), (0, 0, 1, 0), (0, 0, -1, 0), (0, 0, 0, 1)]
    )
    two_hops = peers([(0, 2, 0, 0), (0, -2, 0, 0), (2, 0, 0, 0), (0, 0, 2, 0)])
    four_hops = peers([(0, 4, 0, 0), (0, -4, 0, 0), (0, 0, 0, 1)])
    plane = [(j, 0, i, c) for j in range(ny) for i in range(nx // 2) for c in range(2)]
    line = [(0, i, 0, 0) for i in range(nz)]
    far_first = lambda o: -sum(min(d, n - d) for d, n in zip(o, (ny, nz, nx // 2, 2)))
    groups = [peers(sorted(plane, key=far_first)), peers(sorted(line, key=far_first))]

    loads = [
        pltpu.make_async_copy(src, dst, load_sem.at[i])
        for i, (src, dst) in enumerate(
            [
                (count_hbm, count_ref),
                (weight_hbm, weight_ref),
                (target_hbm, target_ref),
                (source_hbm, source_ref),
                (rhs_hbm, rhs_ref),
                (down_hbm, down_ref),
                (across_hbm, across_ref),
                (anchor_hbm, anchor_ref),
            ]
        )
    ]
    for load in loads:
        load.start()

    barrier = pltpu.get_barrier_semaphore()
    met = [after, before, below, above] + one_hop
    for peer in met:
        pl.semaphore_signal(barrier, inc=1, device_id=peer, device_id_type=MESH)

    def greet(stage, who):
        for peer in who:
            pl.semaphore_signal(greet_sem.at[stage], inc=1, device_id=peer, device_id_type=MESH)

    sent, kept = [], []

    def send(src, dst, peer, index):
        copy = pltpu.make_async_remote_copy(
            src_ref=src,
            dst_ref=dst,
            send_sem=send_sem.at[index],
            recv_sem=recv_sem.at[index],
            device_id=peer,
            device_id_type=MESH,
        )
        copy.start()
        sent.append(copy)
        return copy

    slot = lax.broadcasted_iota(jnp.int32, (1, slots), 1)
    loads[0].wait()
    loads[1].wait()
    live = ((slot < count_ref[0, 0] * BLOCK) & (gz < n_gz - 1)).astype(jnp.float32)
    for k in range(4):
        slot_out[k] = weight_ref[k, 0] * live
    loads[2].wait()
    slot_out[4] = target_ref[0].astype(jnp.float32)
    def post_halo(field, k):
        for c in range(2):
            halo_out[k, 0, c : c + 1, :] = field[c][:1]
            halo_out[k, 1, c : c + 1, :] = field[c][rows - 1 :]
        return [
            send(halo_out.at[k, 0], halo_in.at[k, 0], above, 2 + 4 * k),
            send(halo_out.at[k, 1], halo_in.at[k, 1], below, 3 + 4 * k),
        ]

    pl.semaphore_wait(barrier, len(met))
    copies = [
        send(slot_out, slot_in, after, 0),
    ]
    greet(0, one_hop)

    loads[4].wait()
    field = [rhs_ref[c, 0] for c in range(2)]
    halo = post_halo(field, 0)
    loads[5].wait()
    rim_out[...] = down_ref[0, rows - 1 :]
    copies.append(send(rim_out, rim_in, below, 1))

    low_id = lax.broadcasted_iota(jnp.int32, (LOW, slots), 0)
    place_id = lax.broadcasted_iota(jnp.int32, (highs * rows, slots), 0)

    def split(node):
        col = node & (cols - 1)
        return col & (LOW - 1), (col >> bits_low) * rows + (node >> bits_cols)

    loads[3].wait()
    low, place = split(source_ref[0])
    hot_source[...] = (low_id == low).astype(jnp.float32).astype(jnp.bfloat16)
    mask_source[...] = jnp.where(place_id == place, live, 0.0)


    loads[6].wait()
    loads[7].wait()
    across, down, anchor = across_ref[0], down_ref[0], anchor_ref[0]
    col_id = lax.broadcasted_iota(jnp.int32, (rows, cols), 1)
    row_id = lax.broadcasted_iota(jnp.int32, (rows, cols), 0)
    products = []

    for k in range(ITERS):
        base = 2 + 4 * k
        own = looked_up(pieces(stacked(field), 2), hot_source, [mask_source], 2)
        for c in range(2):
            point_out[k, 0, c : c + 1, :] = own[c]
        own_copy = send(point_out.at[k, 0], point_in.at[k, 0], after, base + 2)
        if k > 0:
            halo = post_halo(field, k)
        right = [jnp.where(col_id == cols - 1, 0.0, pltpu.roll(f, cols - 1, 1)) for f in field]
        if k == 0:
            copies[0].wait_recv()
            low, place = split(slot_in[4].astype(jnp.int32))
            hot_target[...] = (low_id == low).astype(jnp.float32).astype(jnp.bfloat16)
            for mask, one, two in ((mask_left, 0, 2), (mask_right, 1, 3)):
                mask[...] = jnp.where(
                    place_id == place,
                    slot_in[one],
                    jnp.where(place_id == place + 1, slot_in[two], 0.0),
                )
        table = jnp.concatenate([pieces(stacked(field), 2), pieces(stacked(right), 2)], 0)
        there = looked_up(table, hot_target, [mask_left, mask_right], 2)
        for c in range(2):
            point_out[k, 1, c : c + 1, :] = there[c]
        there_copy = send(point_out.at[k, 1], point_in.at[k, 1], before, base + 3)

        image, energy = [], None
        for c in range(2):
            f = field[c]
            gap = f - right[c]
            flux = across * gap
            fall = jnp.where(row_id == rows - 1, 0.0, f - pltpu.roll(f, rows - 1, 0))
            drop = down * fall
            held = anchor * f
            come = jnp.where(col_id == 0, 0.0, pltpu.roll(flux, 1, 1))
            above_me = jnp.where(row_id == 0, 0.0, pltpu.roll(drop, 1, 0))
            image.append(flux - come + drop - above_me + held)
            if k == ITERS - 1:
                term = flux * gap + drop * fall + held * f
                energy = term if energy is None else energy + term
        if k > 0:
            products.append(sum(folded(a * b) for a, b in zip(former, field)))
        products.append(sum(folded(a * a) for a in field))
        if k == ITERS - 1:
            rows_known = [jnp.sum(p, 0, keepdims=True) for p in products]
            energy = folded(energy)

        if k == 0:
            pl.semaphore_wait(greet_sem.at[0], len(one_hop))
            greet(1, two_hops)
        if k == 1:
            pl.semaphore_wait(greet_sem.at[1], len(two_hops))
            greet(2, four_hops)

        def onward():
            own_copy.wait_recv()
            error_in = [there[c] - point_in[k, 0, c : c + 1, :] for c in range(2)]
            left = unstacked(spread(error_in, mask_left, hot_target, 2), rows, highs)
            more = unstacked(spread(error_in, mask_right, hot_target, 2), rows, highs)
            return [a + pltpu.roll(b, 1, 1) for a, b in zip(left, more)]

        if k < ITERS - 1:
            image = [a + b for a, b in zip(image, onward())]

        if k == 0:
            copies[1].wait_recv()
        halo[0].wait_recv()
        halo[1].wait_recv()
        rim = jnp.where(xy > 0, rim_in[...], 0.0)
        for c in range(2):
            f = field[c]
            upper = halo_in[k, 1, c : c + 1, :]
            lower = jnp.where(xy < nx - 1, halo_in[k, 0, c : c + 1, :], 0.0)
            fall = f - lower
            drop = down * fall
            edge = jnp.where(row_id == 0, rim * (f - upper), 0.0)
            image[c] = image[c] + jnp.where(row_id == rows - 1, drop + edge, edge)
            if k == ITERS - 1:
                energy = energy + folded(jnp.where(row_id == rows - 1, drop * fall, 0.0))

        there_copy.wait_recv()
        error = [point_in[k, 1, c : c + 1, :] - own[c] for c in range(2)]
        if k == ITERS - 1:
            tie = sum(e * e for e in error)
            last = jnp.sum(energy, 0, keepdims=True) + folded(tie)
            rows_known.append(last * (1.0 / SCALE))
            rows_known.append(jnp.zeros((8 - MOMENTS, 128), jnp.float32))
            lanes = jnp.concatenate(rows_known, 0)
            eight = lax.broadcasted_iota(jnp.int32, (8, 128), 0)
            total = jnp.sum(lanes, 1, keepdims=True)
            lane = lax.broadcasted_iota(jnp.int32, (8, 128), 1)
            total = jnp.sum(jnp.where(lane == eight, total, 0.0), 0, keepdims=True)

        def post_sum(stage, total):
            sums[stage, 0] = total
            if stage == 0:
                pl.semaphore_wait(greet_sem.at[2], len(four_hops))
            index = 2 + 4 * ITERS + stage
            for i, peer in enumerate(groups[stage]):
                copy = pltpu.make_async_remote_copy(
                    src_ref=sums.at[stage, 0],
                    dst_ref=sums.at[stage, i + 1],
                    send_sem=send_sem.at[index],
                    recv_sem=recv_sem.at[index],
                    device_id=peer,
                    device_id_type=MESH,
                )
                copy.start()

        def take_sum(stage):
            index = 2 + 4 * ITERS + stage
            count = len(groups[stage])
            arrived = sums.at[stage, pl.ds(1, count)]
            pltpu.make_async_copy(arrived, arrived, recv_sem.at[index]).wait()
            return functools.reduce(lambda a, b: a + b, [sums[stage, i] for i in range(count + 1)])

        if k == ITERS - 1:
            post_sum(0, total)
            image = [a + b for a, b in zip(image, onward())]
        back = unstacked(spread(error, mask_source, hot_source, 2), rows, highs)
        latest = [(a - b) * (1.0 / SCALE) for a, b in zip(image, back)]
        for c in range(2):
            basis[k, c] = latest[c]
        keep = pltpu.make_async_copy(basis.at[k], basis_hbm.at[k], keep_sem.at[k])
        keep.start()
        kept.append(keep)
        former, field = field, latest

    post_sum(1, take_sum(0))
    total = take_sum(1)
    lane = lax.broadcasted_iota(jnp.int32, (1, 128), 1)
    mu = [
        jnp.sum(jnp.where(lane == i, total, 0.0), 1, keepdims=True) for i in range(MOMENTS)
    ]
    steps, rest = coefficients(mu)
    rows_of = [jnp.broadcast_to(s, (1, 128)) for s in [s * (1.0 / SCALE) for s in steps] + rest[1:]]
    scalars[...] = jnp.concatenate(rows_of + [jnp.zeros((8 - 2 * ITERS, 128), jnp.float32)], 0)

    for keep in kept:
        keep.wait()
    for copy in sent:
        copy.wait_send()
    for stage in range(2):
        count = len(groups[stage])
        gone = sums.at[stage, pl.ds(1, count)]
        pltpu.make_async_copy(gone, gone, send_sem.at[2 + 4 * ITERS + stage]).wait()


def combine(rhs_hbm, basis_hbm, scalars_hbm, x_hbm, r_hbm, rhs, basis, scalars, x, r, load_sem, save_sem):
    loads = [
        pltpu.make_async_copy(src, dst, load_sem.at[i])
        for i, (src, dst) in enumerate(
            [(scalars_hbm, scalars)]
            + [
                pair
                for c in range(2)
                for pair in ((rhs_hbm.at[c], rhs.at[c]), (basis_hbm.at[:, c], basis.at[:, c]))
            ]
        )
    ]
    for load in loads:
        load.start()
    loads[0].wait()
    values = [scalars[i : i + 1, :1] for i in range(2 * ITERS)]
    saves = []
    for c in range(2):
        loads[1 + 2 * c].wait()
        loads[2 + 2 * c].wait()
        powers = [rhs[c, 0]] + [basis[i, c] for i in range(ITERS)]
        x[c, 0] = sum(s * v for s, v in zip(values[:ITERS], powers))
        r[c, 0] = powers[0] + sum(s * v for s, v in zip(values[ITERS:], powers[1:]))
        for n, (src, dst) in enumerate(((x, x_hbm), (r, r_hbm))):
            save = pltpu.make_async_copy(src.at[c], dst.at[c], save_sem.at[2 * c + n])
            save.start()
            saves.append(save)
    for save in saves:
        save.wait()


def body(nz, rhs, across, down, anchor, source, target, weight, count):
    n_gz, nx = lax.axis_size("gz"), lax.axis_size("xy")
    ny = n_gz // nz
    rows, cols = across.shape[1:]
    slots = source.shape[2]
    places = rows * cols // LOW
    f32, bf16 = jnp.float32, jnp.bfloat16
    vmem = pl.BlockSpec(memory_space=pltpu.VMEM)
    hbm = pl.BlockSpec(memory_space=pltpu.HBM)
    args = (rhs, across, down, anchor, source, target, weight, count)
    copies = 2 + 4 * ITERS + 2
    widest = max(nx * ny, nz)
    basis, scalars = pl.pallas_call(
        functools.partial(kernel, ny, nz, nx),
        out_shape=(
            jax.ShapeDtypeStruct((ITERS, 2, rows, cols), f32),
            jax.ShapeDtypeStruct((8, 128), f32),
        ),
        in_specs=[hbm] * len(args),
        out_specs=(hbm, vmem),
        scratch_shapes=[
            pltpu.VMEM(rhs.shape, f32),
            pltpu.VMEM(across.shape, f32),
            pltpu.VMEM(down.shape, f32),
            pltpu.VMEM(anchor.shape, f32),
            pltpu.VMEM(source.shape, jnp.int32),
            pltpu.VMEM(target.shape, jnp.int32),
            pltpu.VMEM(weight.shape, f32),
            pltpu.SMEM(count.shape, jnp.int32),
            pltpu.VMEM((LOW, slots), bf16),
            pltpu.VMEM((LOW, slots), bf16),
            pltpu.VMEM((places, slots), f32),
            pltpu.VMEM((places, slots), f32),
            pltpu.VMEM((places, slots), f32),
            pltpu.VMEM((ITERS, 2, rows, cols), f32),
            pltpu.VMEM((5, 1, slots), f32),
            pltpu.VMEM((1, cols), f32),
            pltpu.VMEM((ITERS, 2, 2, cols), f32),
            pltpu.VMEM((ITERS, 2, 2, slots), f32),
            pltpu.VMEM((5, 1, slots), f32),
            pltpu.VMEM((1, cols), f32),
            pltpu.VMEM((ITERS, 2, 2, cols), f32),
            pltpu.VMEM((ITERS, 2, 2, slots), f32),
            pltpu.VMEM((2, widest, 1, 128), f32),
            pltpu.SemaphoreType.DMA((copies,)),
            pltpu.SemaphoreType.DMA((copies,)),
            pltpu.SemaphoreType.DMA((8,)),
            pltpu.SemaphoreType.DMA((ITERS,)),
            pltpu.SemaphoreType.REGULAR((3,)),
        ],
        compiler_params=pltpu.CompilerParams(
            collective_id=0, has_side_effects=True, vmem_limit_bytes=63 * 1024 * 1024
        ),
    )(*args)
    out = jax.ShapeDtypeStruct(rhs.shape, f32)
    return pl.pallas_call(
        combine,
        out_shape=(out, out),
        in_specs=[hbm] * 3,
        out_specs=(hbm, hbm),
        scratch_shapes=[
            pltpu.VMEM(rhs.shape, f32),
            pltpu.VMEM(basis.shape, f32),
            pltpu.VMEM(scalars.shape, f32),
            pltpu.VMEM(rhs.shape, f32),
            pltpu.VMEM(rhs.shape, f32),
            pltpu.SemaphoreType.DMA((5,)),
            pltpu.SemaphoreType.DMA((4,)),
        ],
        compiler_params=pltpu.CompilerParams(vmem_limit_bytes=63 * 1024 * 1024),
    )(rhs, basis, scalars)


def solution(mesh, nz=16):
    in_specs = (
        P(None, "gz", "xy", None),
        P("gz", "xy", None),
        P("gz", "xy", None),
        P("gz", "xy", None),
        P("gz", "xy", None),
        P("gz", "xy", None),
        P(None, "gz", "xy", None),
        P("gz", "xy"),
    )
    out_specs = (P(None, "gz", "xy", None), P(None, "gz", "xy", None))
    return jax.shard_map(
        functools.partial(body, nz), mesh=mesh, in_specs=in_specs, out_specs=out_specs, check_vma=False
    )
```
